32 devices in a mesh: ctx: 4 (over z), mp: 4 (over y, core), rep: 2 (over x).
Axes of the slice: x: 2, y: 2, z: 4, core: 2. Of those that a mesh axis runs over, the one named last changes fastest.
Arguments:
- token_pages: bfloat16 [32, 128, 2048], P('ctx'), may hold values from -13 to 13
- page_table: int32 [32], P('ctx'), may hold values from 0 to 7, as said below
- live_flags: int32 [32], P('ctx'), may hold values from 0 to 1, as said below
- lengths: int32 [32], replicated, may hold values from 1 to 256, as said below
- decay_floor: float32 [2048], P(('mp', 'rep')), may hold values from 0.85 to 0.9998
- mixer_gain: float32 [2048], replicated, may hold values from 0.5 to 1.5
- feed_gain: float32 [2048], replicated, may hold values from 0.5 to 1.5
- trainer_mixer_in: float32 [3, 2048, 2048], P(None, ('ctx', 'mp')), may hold values from -0.125 to 0.125
- trainer_mixer_out: float32 [2048, 2048], P(None, ('ctx', 'mp')), may hold values from -0.125 to 0.125
- trainer_gate_up: float32 [2, 2048, 5632], P(None, ('ctx', 'mp')), may hold values from -0.125 to 0.125
- trainer_down: float32 [5632, 2048], P(None, ('ctx', 'mp')), may hold values from -0.078125 to 0.078125
Outputs:
- layer_output: bfloat16 [4096, 2048], P(('ctx', 'rep'), 'mp')
The draws below stay inside these ranges and needn't reach their ends.
Inputs may be any that keep to these rules, and one draw needn't show every extreme that they name: `page_table`: within each device's block of 8 entries every value 0 to 7 appears once. `live_flags`: in each device's block of 8 flags at least half (rounded down, and never fewer than one) are ones, and some device's block is all ones. The lengths sum to 128 times the number of ones in live_flags; one prompt has exactly 256 tokens.
All inputs are finite; a program needn't handle non-finite values.
Results may differ from the reference program's by a relative error of at most 0.015.
Values may be sent and summed in bfloat16 or wider, within the bound.
No kernel may reach another device: no remote copies, remote signals or barrier semaphores. Data moves between devices by JAX's collectives and lax.ppermute only.
A program may use at most 192 MiB of HBM per device.

```python
import math
import jax
import jax.numpy as jnp
from jax import lax

D = 2048
HEADS = 16
FF = 5632
PAGE = 128
PAGES_DEV = 8
PROMPTS = 32
TOKENS = 4096
PAGES = 32
N_CTX = 4


def pages_and_lengths(key):
    folded = jax.random.fold_in(key, 91)
    key_count, key_full, key_rank, key_shift, key_roll = jax.random.split(folded, 5)
    groups = PAGES // PAGES_DEV
    counts = jax.random.randint(key_count, (groups,), max(1, PAGES_DEV // 2), PAGES_DEV + 1).astype(jnp.int32)
    full_one = jax.random.randint(key_full, (), 0, groups)
    counts = jnp.where(jnp.arange(groups) == full_one, PAGES_DEV, counts).astype(jnp.int32)
    ranking = jax.vmap(lambda subkey: jax.random.permutation(subkey, PAGES_DEV))(jax.random.split(key_rank, groups))
    live_marks = (ranking < counts[:, None]).astype(jnp.int32).reshape(PAGES)
    live_total = (jnp.sum(counts) * PAGE).astype(jnp.int32)
    longest = 2 * TOKENS // PROMPTS
    others = PROMPTS - 1
    rest = (live_total - longest).astype(jnp.int32)
    share = (rest // others).astype(jnp.int32)
    extra = (rest % others).astype(jnp.int32)
    slots = jnp.arange(others, dtype=jnp.int32)
    base = (share + (slots < extra).astype(jnp.int32)).astype(jnp.int32)
    pairs = others // 2
    reach = (share // 2).astype(jnp.int32)
    unit = jax.random.randint(key_shift, (pairs,), 0, 1 << 20).astype(jnp.int32)
    shift = (unit % (2 * reach + 1) - reach).astype(jnp.int32)
    moved = jnp.zeros((others,), jnp.int32)
    moved = moved.at[0:2 * pairs:2].set(shift).at[1:2 * pairs:2].set(-shift)
    rest_lengths = (base + moved).astype(jnp.int32)
    lengths = jnp.concatenate([jnp.full((1,), longest, jnp.int32), rest_lengths])
    offset = jax.random.randint(key_roll, (), 0, PROMPTS)
    lengths = jnp.roll(lengths, offset).astype(jnp.int32)
    return (live_marks, lengths)


def draw_live_flags(key, part):
    return pages_and_lengths(key)[0]


def draw_lengths(key, part):
    return pages_and_lengths(key)[1]


def draw_page_table(key, part):
    groups = PAGES // PAGES_DEV
    subkeys = jax.random.split(jax.random.fold_in(key, 17), groups)
    ranking = jax.vmap(lambda subkey: jax.random.permutation(subkey, PAGES_DEV))(subkeys)
    return ranking.astype(jnp.int32).reshape(PAGES)


def draw_decay_floor(key, part):
    key_level, key_jitter = jax.random.split(jax.random.fold_in(key, 23))
    head_dim = D // HEADS
    head_level = jax.random.uniform(key_level, (HEADS, 1), jnp.float32, 0.0, 1.0)
    lowest_log = math.log(0.0003)
    highest_log = math.log(0.1)
    jitter = jnp.exp(jax.random.uniform(key_jitter, (HEADS, head_dim), jnp.float32, -0.35, 0.35))
    return (1.0 - jnp.exp(lowest_log + head_level * (highest_log - lowest_log)) * jitter).reshape(D)


def draw_token_pages(key, part):
    key_scale, key_values = jax.random.split(jax.random.fold_in(key, 5), 2)
    scales = 0.3 * jnp.exp(jax.random.uniform(key_scale, (PAGES, PAGE, 1), jnp.float32, 0.0, math.log(10.0)))
    entries = jnp.clip(jax.random.normal(key_values, (PAGES, PAGE, D), jnp.float32), -4.0, 4.0)
    return (scales * entries).astype(jnp.bfloat16)


def block_levels(stream_key, dims, cuts, smallest, top_value):
    loudness, own = 1.0, jax.random.fold_in(stream_key, 6)
    for dim, shards_of in cuts:
        heights = jnp.exp(jax.random.uniform(jax.random.fold_in(own, dim), (shards_of,), jnp.float32, smallest / len(cuts), top_value / len(cuts)))
        loudness = loudness * jnp.repeat(heights, dims[dim] // shards_of).reshape([-1 if axis == dim else 1 for axis in range(len(dims))])
    return loudness


def gaussian(key, shape, scale, bound, cuts=(), kind=jnp.bfloat16):
    drawn = scale * jax.random.normal(key, shape, jnp.float32)
    if cuts:
        drawn = drawn * block_levels(key, shape, cuts, -0.22, 0.18)
    return jnp.clip(drawn, -bound, bound).astype(kind)


def setup_inputs(seed: int = 0) -> dict:
    splits = jax.random.split(jax.random.key(seed), 12)
    token_pages = draw_token_pages(jax.random.fold_in(splits[11], 71), 0)
    page_table = draw_page_table(jax.random.fold_in(splits[11], 71), 0)
    live_flags = draw_live_flags(jax.random.fold_in(splits[11], 71), 0)
    lengths = draw_lengths(jax.random.fold_in(splits[11], 71), 0)
    decay_floor = draw_decay_floor(jax.random.fold_in(splits[11], 71), 0)
    mixer_gain = jnp.clip(1.0 + 0.1 * jax.random.normal(splits[5], (D,), jnp.float32), 0.5, 1.5)
    feed_gain = jnp.clip(1.0 + 0.1 * jax.random.normal(splits[6], (D,), jnp.float32), 0.5, 1.5)
    trainer_mixer_in = gaussian(splits[7], (3, D, D), D ** -0.5, 0.125, ((1, 16),), jnp.float32)
    trainer_mixer_out = gaussian(splits[8], (D, D), D ** -0.5, 0.125, ((1, 16),), jnp.float32)
    trainer_gate_up = gaussian(splits[9], (2, D, FF), D ** -0.5, 0.125, ((1, 16),), jnp.float32)
    trainer_down = gaussian(splits[10], (FF, D), FF ** -0.5, 0.078125, ((1, 16),), jnp.float32)
    return {"token_pages": token_pages, "page_table": page_table, "live_flags": live_flags, "lengths": lengths, "decay_floor": decay_floor, "mixer_gain": mixer_gain, "feed_gain": feed_gain, "trainer_mixer_in": trainer_mixer_in, "trainer_mixer_out": trainer_mixer_out, "trainer_gate_up": trainer_gate_up, "trainer_down": trainer_down}


norm_eps = 1e-05

def rms_scale(values_in, gain):
    mean_sq = lax.optimization_barrier(jnp.mean(values_in * values_in, axis=-1, keepdims=True))
    return values_in * lax.rsqrt(mean_sq + norm_eps) * gain

def block_recurrence(queries, keys_in, values_in, log_decay, reset_count, state_init, count_init):
    highest = lax.Precision.HIGHEST

    def advance(carried_in, block_data):
        state, count_before = carried_in
        q_block, k_block, v_block, decay_block, count_block = block_data
        cumulative = jnp.cumsum(decay_block, axis=0)
        q_scaled = q_block * jnp.exp(cumulative)
        k_scaled = k_block * jnp.exp(-cumulative)
        scores = jnp.einsum('thd,shd->hts', q_scaled, k_scaled, precision=highest)
        positions = jnp.arange(count_block.shape[0])
        allowed = (positions[:, None] >= positions[None, :]) & (count_block[:, None] == count_block[None, :])
        scores = jnp.where(allowed[None], scores, 0.0)
        outputs = jnp.einsum('hts,shd->thd', scores, v_block, precision=highest)
        from_state = jnp.einsum('thd,hde->the', q_scaled, state, precision=highest)
        outputs = outputs + jnp.where((count_block == count_before)[:, None, None], from_state, 0.0)
        last_count = count_block[-1]
        final_cum = cumulative[-1]
        weight_keys = k_block * jnp.exp(final_cum[None] - cumulative) * (count_block == last_count).astype(k_block.dtype)[:, None, None]
        retained = jnp.where(last_count == count_before, jnp.exp(final_cum)[:, :, None] * state, 0.0)
        state_next = retained + jnp.einsum('thd,the->hde', weight_keys, v_block, precision=highest)
        return ((state_next, last_count), outputs)
    final_carry, outputs_all = lax.scan(advance, (state_init, count_init), (queries, keys_in, values_in, log_decay, reset_count))
    return (outputs_all, final_carry[0])

def reference(token_pages, page_table, live_flags, lengths, decay_floor, mixer_gain, feed_gain, trainer_mixer_in, trainer_mixer_out, trainer_gate_up, trainer_down):
    head_dim = D // HEADS
    table = page_table.reshape(N_CTX, PAGES_DEV).astype(jnp.int32)
    paged = token_pages.reshape(N_CTX, PAGES_DEV, PAGE, D)
    ordered = jnp.take_along_axis(paged, table[:, :, None, None], axis=1).reshape(TOKENS, D)
    live_tokens = jnp.repeat(live_flags, PAGE).astype(jnp.int32)
    before = (jnp.cumsum(live_tokens) - live_tokens).astype(jnp.int32)
    starts = (jnp.cumsum(lengths) - lengths).astype(jnp.int32)
    resets = (live_tokens == 1) & jnp.any(before[:, None] == starts[None, :], axis=1)
    reset_count = jnp.cumsum(resets.astype(jnp.int32)).astype(jnp.int32)
    live_float = live_tokens.astype(jnp.float32)[:, None]
    w_query = trainer_mixer_in[0].astype(jnp.bfloat16)
    w_forget = trainer_mixer_in[1].astype(jnp.bfloat16)
    w_value = trainer_mixer_in[2].astype(jnp.bfloat16)
    w_output = trainer_mixer_out.astype(jnp.bfloat16)
    w_gate = trainer_gate_up[0].astype(jnp.bfloat16)
    w_up = trainer_gate_up[1].astype(jnp.bfloat16)
    w_down = trainer_down.astype(jnp.bfloat16)
    normed = rms_scale(ordered.astype(jnp.float32), mixer_gain).astype(jnp.bfloat16)
    queries = jax.nn.silu(jnp.dot(normed, w_query, preferred_element_type=jnp.float32))
    forget = decay_floor + (1.0 - decay_floor) * jax.nn.sigmoid(jnp.dot(normed, w_forget, preferred_element_type=jnp.float32))
    log_decay = jnp.log(forget) * live_float
    keys_in = (1.0 - forget) * live_float
    values_in = jnp.dot(normed, w_value, preferred_element_type=jnp.float32)
    blocks = TOKENS // PAGE
    shape_blocks = (blocks, PAGE, HEADS, head_dim)
    outputs_all, unused_state = block_recurrence(queries.reshape(shape_blocks), keys_in.reshape(shape_blocks), values_in.reshape(shape_blocks), log_decay.reshape(shape_blocks), reset_count.reshape(blocks, PAGE), jnp.zeros((HEADS, head_dim, head_dim), jnp.float32), jnp.zeros((), jnp.int32))
    mixed = outputs_all.reshape(TOKENS, HEADS, head_dim)
    head_normed = (mixed * lax.rsqrt(lax.optimization_barrier(jnp.mean(mixed * mixed, axis=-1, keepdims=True)) + norm_eps)).reshape(TOKENS, D).astype(jnp.bfloat16)
    residual = ordered.astype(jnp.float32) + jnp.dot(head_normed, w_output, preferred_element_type=jnp.float32)
    feed_in = rms_scale(residual, feed_gain).astype(jnp.bfloat16)
    gate = jnp.dot(feed_in, w_gate, preferred_element_type=jnp.float32)
    upward = jnp.dot(feed_in, w_up, preferred_element_type=jnp.float32)
    hidden = (jax.nn.silu(gate) * upward).astype(jnp.bfloat16)
    result = residual + jnp.dot(hidden, w_down, preferred_element_type=jnp.float32)
    return jnp.where(live_tokens[:, None] == 1, result, 0.0).astype(jnp.bfloat16)
```

```python
import functools

import jax
import jax.numpy as jnp
from jax import lax
from jax.experimental import pallas as pl
from jax.experimental.pallas import tpu as pltpu
from jax.sharding import PartitionSpec as P

HEAD = 128
EPS = 1e-05
BF = jnp.bfloat16
F32 = jnp.float32
VMEM_LIMIT = 48 * 1024 * 1024


def nt(a, b):
    return lax.dot_general(a, b, (((1,), (1,)), ((), ())), preferred_element_type=F32)


def tn(a, b):
    return lax.dot_general(a, b, (((0,), (0,)), ((), ())), preferred_element_type=F32)


def nn(a, b):
    return jnp.dot(a, b, preferred_element_type=F32)


def sigmoid(v):
    return 1.0 / (1.0 + jnp.exp(-v))


def call(body, grid, in_specs, out_specs, out_shape, scratch=(), prefetch=1, cost=None):
    return pl.pallas_call(
        body,
        out_shape=out_shape,
        grid_spec=pltpu.PrefetchScalarGridSpec(
            num_scalar_prefetch=prefetch,
            grid=grid,
            in_specs=in_specs,
            out_specs=out_specs,
            scratch_shapes=list(scratch),
        ),
        compiler_params=pltpu.CompilerParams(
            dimension_semantics=("arbitrary",) * len(grid), vmem_limit_bytes=VMEM_LIMIT
        ),
        cost_estimate=None
        if cost is None
        else pl.CostEstimate(flops=cost[0], bytes_accessed=cost[1], transcendentals=0),
    )


def whole(shape):
    zeros = (0,) * len(shape)
    return pl.BlockSpec(shape, lambda *_: zeros, pipeline_mode=pl.Buffered(1))


def pack_mixer(ids, mixer_in, mixer_out):
    width = mixer_in.shape[1]
    cols = mixer_in.shape[2] // 8

    def body(ids_ref, q_ref, f_ref, v_ref, o_ref, out_ref):
        out_ref[0, :, 0:cols] = q_ref[0].astype(BF)
        out_ref[0, :, cols : 2 * cols] = f_ref[0].astype(BF)
        out_ref[0, :, 2 * cols : 3 * cols] = v_ref[0].astype(BF)
        out_ref[0, :, 3 * cols : 4 * cols] = o_ref[...].T.astype(BF)

    def dest(s, ids_ref):
        return 2 * (ids_ref[0] ^ s) + ids_ref[1]

    def part(i):
        return pl.BlockSpec((1, width, cols), lambda s, r: (i, 0, dest(s, r)))

    return call(
        body,
        (4,),
        [part(0), part(1), part(2), pl.BlockSpec((cols, width), lambda s, r: (dest(s, r), 0))],
        pl.BlockSpec((1, width, 4 * cols), lambda s, r: (s, 0, 0)),
        jax.ShapeDtypeStruct((4, width, 4 * cols), BF),
        cost=(0, 4 * width * cols * 24),
    )(ids, mixer_in, mixer_in, mixer_in, mixer_out)


def feed_sizes(hidden_all):
    full = hidden_all // 128 // 8 * 128
    half = (hidden_all - 8 * full) // 8
    return full, half


def pack_feed(ids, gate_up, down):
    width = gate_up.shape[1]
    full, half = feed_sizes(gate_up.shape[2])
    assert half == 64
    gu = 2 * full + 128
    total = gu + full + 128

    def body(ids_ref, g_ref, u_ref, gh_ref, uh_ref, d_ref, dh_ref, out_ref):
        odd = (ids_ref[0] ^ pl.program_id(0)) % 2
        out_ref[0, :, 0:full] = g_ref[0].astype(BF)
        lane = lax.broadcasted_iota(jnp.int32, (width, 128), 1)
        gh, uh = gh_ref[0], uh_ref[0]
        even_mix = jnp.where(lane < 64, gh, pltpu.roll(uh, 64, 1))
        odd_mix = jnp.where(lane < 64, pltpu.roll(gh, 64, 1), uh)
        out_ref[0, :, full : full + 128] = jnp.where(odd == 1, odd_mix, even_mix).astype(BF)
        out_ref[0, :, full + 128 : gu] = u_ref[0].astype(BF)
        out_ref[0, :, gu : gu + full] = d_ref[...].T.astype(BF)
        last = jnp.concatenate([dh_ref[...], jnp.zeros((64, width), F32)], axis=0)
        out_ref[0, :, gu + full : total] = last.T.astype(BF)

    def dest(s, r):
        return 4 * r[1] + (r[0] ^ s)

    def tile(s, r):
        return 8 * full // 128 + 2 * r[1] + (r[0] ^ s) // 2

    def cols(i):
        return pl.BlockSpec((1, width, full), lambda s, r: (i, 0, dest(s, r)))

    def mix(i):
        return pl.BlockSpec((1, width, 128), lambda s, r: (i, 0, tile(s, r)))

    return call(
        body,
        (4,),
        [
            cols(0),
            cols(1),
            mix(0),
            mix(1),
            pl.BlockSpec((full, width), lambda s, r: (dest(s, r), 0)),
            pl.BlockSpec((64, width), lambda s, r: (8 * full // 64 + dest(s, r), 0)),
        ],
        pl.BlockSpec((1, width, total), lambda s, r: (s, 0, 0)),
        jax.ShapeDtypeStruct((4, width, total), BF),
        cost=(0, 4 * width * total * 6),
    )(ids, gate_up, gate_up, gate_up, gate_up, down, down)


def mp_perm(value, s):
    return lax.ppermute(value, "mp", [(i, i ^ s) for i in range(4)])


def rep_perm(value):
    return lax.ppermute(value, "rep", [(0, 1), (1, 0)])


def across_plane(packed, mp_index):
    arrived = [packed[0]] + [mp_perm(packed[s], s) for s in (1, 2, 3)]
    out = jnp.zeros(packed.shape, packed.dtype)
    for s in range(4):
        out = lax.dynamic_update_index_in_dim(out, arrived[s], mp_index ^ s, 0)
    return out.reshape(4 * packed.shape[1], packed.shape[2])


def along_line(block, ctx_index, count):
    if count != 4:
        return lax.all_gather(block, "ctx", axis=0)
    out = jnp.zeros((3 * count - 2, *block.shape), block.dtype)
    out = lax.dynamic_update_index_in_dim(out, block, ctx_index + count - 1, 0)
    low = high = block
    for d in range(1, count):
        low = lax.ppermute(low, "ctx", [(i, i + 1) for i in range(count - 1)])
        high = lax.ppermute(high, "ctx", [(i + 1, i) for i in range(count - 1)])
        out = lax.dynamic_update_index_in_dim(out, low, ctx_index - d + count - 1, 0)
        out = lax.dynamic_update_index_in_dim(out, high, ctx_index + d + count - 1, 0)
    return out[count - 1 : 2 * count - 1]


def from_earlier(value, count):
    return [
        lax.ppermute(value, "ctx", [(i, i + d) for i in range(count - d)]) for d in range(1, count)
    ]


def normalise(page_table, token_pages, gain):
    pages, page, width = token_pages.shape

    def body(table_ref, x_ref, g_ref, out_ref):
        x = x_ref[0].astype(F32)
        scale = lax.rsqrt(jnp.mean(x * x, axis=-1, keepdims=True) + EPS)
        out_ref[...] = (x * scale * g_ref[...]).astype(BF)

    return call(
        body,
        (pages,),
        [pl.BlockSpec((1, page, width), lambda i, t: (t[i], 0, 0)), whole((1, width))],
        pl.BlockSpec((page, width), lambda i, t: (i, 0)),
        jax.ShapeDtypeStruct((pages * page, width), BF),
        cost=(pages * page * width * 4, pages * page * width * 4),
    )(page_table, token_pages, gain.reshape(1, width))


def step_state(state, ks, v, same_last, keep, final):
    update = tn(v, jnp.where(same_last, ks, jnp.zeros_like(ks)))
    return (jnp.where(keep, state, 0.0) + update) * final


def project(live, last, normed, weights, floor, cnt_col):
    rows, width = normed.shape
    cols = floor.shape[1]
    heads = cols // HEAD
    pages = live.shape[0]
    page = rows // pages
    group = 2
    steps = pages // group

    def body(live_ref, last_ref, x_ref, w_ref, fl_ref, cnt_ref, qs_ref, ks_ref, v_ref, fin_ref, st_ref, state, total):
        step = pl.program_id(0)

        @pl.when(step == 0)
        def _():
            state[...] = jnp.zeros_like(state)
            total[...] = jnp.zeros_like(total)

        proj = nn(x_ref[...], w_ref[:, 0 : 3 * cols])
        row = lax.broadcasted_iota(jnp.int32, (page, page), 0)
        col = lax.broadcasted_iota(jnp.int32, (page, page), 1)
        lower = (row >= col).astype(F32)
        floor_row = fl_ref[...]
        for j in range(group):
            p = step * group + j
            here = slice(j * page, (j + 1) * page)
            alive = live_ref[p].astype(F32)
            now = last_ref[p]
            before = jnp.where(p == 0, 0, last_ref[jnp.maximum(p - 1, 0)])
            q = proj[here, 0:cols]
            q = q * sigmoid(q)
            f = proj[here, cols : 2 * cols]
            gate = sigmoid(f)
            forget = floor_row + (1.0 - floor_row) * gate
            key = (1.0 - forget) * alive
            log_decay = jnp.log(forget) * alive
            cum = jnp.dot(lower, log_decay, precision=lax.Precision.HIGHEST, preferred_element_type=F32)
            final_log = cum[page - 1 : page, :]
            final = jnp.exp(final_log)
            ks = (key * jnp.exp(-cum)).astype(BF)
            v = proj[here, 2 * cols : 3 * cols].astype(BF)
            qs_ref[here, :] = (q * jnp.exp(cum)).astype(BF)
            ks_ref[here, :] = ks
            v_ref[here, :] = v
            fin_ref[j] = final
            total[...] += final_log
            same_last = cnt_ref[here, :] == now
            for h in range(heads):
                hc = slice(h * HEAD, (h + 1) * HEAD)
                state[h] = step_state(state[h], ks[:, hc], v[:, hc], same_last, now == before, final[:, hc])

        @pl.when(step == steps - 1)
        def _():
            none = last_ref[pages - 1] == 0
            decay = jnp.where(none, jnp.exp(total[...]), 0.0)
            for h in range(heads):
                st_ref[h, 0:HEAD, :] = state[h].astype(BF)
                st_ref[h, HEAD : HEAD + 16, :] = jnp.broadcast_to(
                    decay[:, h * HEAD : (h + 1) * HEAD], (16, HEAD)
                ).astype(BF)

    block = group * page
    return call(
        body,
        (steps,),
        [
            pl.BlockSpec((block, width), lambda i, *_: (i, 0)),
            whole((width, weights.shape[1])),
            whole((1, cols)),
            pl.BlockSpec((block, 1), lambda i, *_: (i, 0)),
        ],
        [
            pl.BlockSpec((block, cols), lambda i, *_: (i, 0)),
            pl.BlockSpec((block, cols), lambda i, *_: (i, 0)),
            pl.BlockSpec((block, cols), lambda i, *_: (i, 0)),
            pl.BlockSpec((group, 1, cols), lambda i, *_: (i, 0, 0)),
            whole((heads, HEAD + 16, HEAD)),
        ],
        [
            jax.ShapeDtypeStruct((rows, cols), BF),
            jax.ShapeDtypeStruct((rows, cols), BF),
            jax.ShapeDtypeStruct((rows, cols), BF),
            jax.ShapeDtypeStruct((pages, 1, cols), F32),
            jax.ShapeDtypeStruct((heads, HEAD + 16, HEAD), BF),
        ],
        scratch=[pltpu.VMEM((heads, HEAD, HEAD), F32), pltpu.VMEM((1, cols), F32)],
        prefetch=2,
        cost=(2 * rows * width * 3 * cols, rows * width * 2 + width * cols * 8),
    )(live, last, normed, weights, floor, cnt_col)


def mix(last, ids, earlier, qs, ks, v, fin, weights, cnt_col, cnt_row):
    rows, cols = qs.shape
    heads = cols // HEAD
    pages = fin.shape[0]
    page = rows // pages
    group = 2
    steps = pages // group
    width = weights.shape[1] * 4
    n = len(earlier)

    def body(last_ref, ids_ref, *refs):
        packs = refs[:n]
        qs_ref, ks_ref, v_ref, fin_ref, w_ref, cc_ref, cr_ref, out_ref, state = refs[n:]
        step = pl.program_id(0)
        mp_index = ids_ref[0]

        @pl.when(step == 0)
        def _():
            for h in range(heads):
                total = jnp.zeros((HEAD, HEAD), F32)
                for pack in reversed(packs):
                    total = total * pack[h, HEAD : HEAD + 1, :].astype(F32) + pack[h, 0:HEAD, :].astype(F32)
                state[h] = total

        row = lax.broadcasted_iota(jnp.int32, (page, page), 0)
        col = lax.broadcasted_iota(jnp.int32, (page, page), 1)
        lower = row >= col
        normed = []
        for j in range(group):
            p = step * group + j
            here = slice(j * page, (j + 1) * page)
            now = last_ref[p]
            before = jnp.where(p == 0, 0, last_ref[jnp.maximum(p - 1, 0)])
            cc, cr = cc_ref[here, :], cr_ref[j]
            allowed = lower & (cc == cr)
            reached = cc == before
            same_last = cc == now
            for h in range(heads):
                hc = slice(h * HEAD, (h + 1) * HEAD)
                q_h, k_h, v_h = qs_ref[here, hc], ks_ref[here, hc], v_ref[here, hc]
                scores = jnp.where(allowed, nt(q_h, k_h), 0.0).astype(BF)
                out = nn(scores, v_h)
                out = out + jnp.where(reached, nt(q_h, state[h].astype(BF)), 0.0)
                state[h] = step_state(state[h], k_h, v_h, same_last, now == before, fin_ref[j, :, hc])
                scale = lax.rsqrt(jnp.mean(out * out, axis=-1, keepdims=True) + EPS)
                normed.append((out * scale).astype(BF))
        hn = jnp.concatenate(
            [jnp.concatenate(normed[j * heads : (j + 1) * heads], axis=1) for j in range(group)], axis=0
        )
        for dc in range(2):
            for dy in range(2):
                w = w_ref[mp_index ^ (2 * dy + dc)]
                out_ref[dc, 0, 0, dy] = nt(hn, w[:, 3 * cols : 4 * cols]).astype(BF)

    block = group * page
    rowspec = pl.BlockSpec((block, cols), lambda i, *_: (i, 0))
    return call(
        body,
        (steps,),
        [whole(e.shape) for e in earlier]
        + [
            rowspec,
            rowspec,
            rowspec,
            pl.BlockSpec((group, 1, cols), lambda i, *_: (i, 0, 0)),
            whole(weights.shape),
            pl.BlockSpec((block, 1), lambda i, *_: (i, 0)),
            pl.BlockSpec((group, 1, page), lambda i, *_: (i, 0, 0)),
        ],
        pl.BlockSpec(
            (2, 1, 1, 2, block, width // 4), lambda i, l, r: (0, i % 2, (i // 2) ^ r[1], 0, 0, 0)
        ),
        jax.ShapeDtypeStruct((2, 2, 2, 2, block, width // 4), BF),
        scratch=[pltpu.VMEM((heads, HEAD, HEAD), F32)],
        prefetch=2,
        cost=(2 * rows * cols * width, rows * width * 2),
    )(last, ids, *earlier, qs, ks, v, fin, weights, cnt_col, cnt_row)


def add(a, b):
    return (a.astype(F32) + b.astype(F32)).astype(BF)


def sum_scatter(terms):
    total = add(terms[0], mp_perm(terms[1], 1))
    a_first = add(total[0, 0], rep_perm(total[0, 1]))
    b_first = add(total[1, :, 0], mp_perm(total[1, :, 1], 2))
    a = a_first[0].astype(F32) + mp_perm(a_first[1], 2).astype(F32)
    b = b_first[0].astype(F32) + rep_perm(b_first[1]).astype(F32)
    return jnp.concatenate([a, b], axis=0)


def gather_plane(value):
    half = value.shape[0] // 2
    a, b = value[:half], value[half:]
    a_y, b_x = mp_perm(a, 2), rep_perm(b)
    a_pair, b_pair = jnp.stack([a, a_y]), jnp.stack([b, b_x])
    a_x, b_y = rep_perm(a_pair), mp_perm(b_pair, 2)
    mine = jnp.stack([jnp.stack([a_pair, a_x]), jnp.stack([b_pair, b_y], axis=1)])
    return mine, mp_perm(mine, 1)


def feed_forward(ids, mine, other, gain, weights, full):
    rows, kwide = mine.shape[-2:]
    total = weights.shape[2]
    gu = 2 * full + 128

    def body(ids_ref, m_ref, o_ref, g_ref, w_ref, out_ref):
        mp_index = ids_ref[0]
        places = [(dy, dc) for dy in range(2) for dc in range(2)]
        blocks = [(m_ref, o_ref)[dc][0, 0, dy].astype(F32) for dy, dc in places]
        square = sum(jnp.sum(b * b, axis=-1, keepdims=True) for b in blocks)
        scale = lax.rsqrt(square / (4 * kwide) + EPS)
        h = None
        for (dy, dc), b in zip(places, blocks):
            k = mp_index ^ (2 * dy + dc)
            x = (b * scale * g_ref[k]).astype(BF)
            term = nn(x, w_ref[k, :, 0:gu])
            h = term if h is None else h + term
        gate, up = h[:, 0:full], h[:, full + 128 : gu]
        edge = h[:, full : full + 128]
        hidden = gate * sigmoid(gate) * up
        mixed = edge * sigmoid(edge) * pltpu.roll(edge, 64, 1)
        lane = lax.broadcasted_iota(jnp.int32, mixed.shape, 1)
        mixed = jnp.where(lane < 64, mixed, 0.0)
        hidden = jnp.concatenate([hidden, mixed], axis=1).astype(BF)
        for dy, dc in places:
            k = mp_index ^ (2 * dy + dc)
            out_ref[dc, 0, 0, dy] = nt(hidden, w_ref[k, :, gu:total]).astype(BF)

    spec = pl.BlockSpec((1, 1, 2, rows, kwide), lambda i, r: (i % 2, i // 2, 0, 0, 0))
    return call(
        body,
        (4,),
        [spec, spec, whole(gain.shape), whole(weights.shape)],
        pl.BlockSpec((2, 1, 1, 2, rows, kwide), lambda i, r: (0, i % 2, i // 2, 0, 0, 0)),
        jax.ShapeDtypeStruct((2, 2, 2, 2, rows, kwide), BF),
        cost=(2 * 4 * rows * 4 * kwide * total, 4 * kwide * total * 2 + 32 * rows * kwide * 2),
    )(ids, mine, other, gain, weights)


def shards(
    token_pages,
    page_table,
    live_flags,
    lengths,
    decay_floor,
    mixer_gain,
    feed_gain,
    trainer_mixer_in,
    trainer_mixer_out,
    trainer_gate_up,
    trainer_down,
):
    ctx_count = lax.axis_size("ctx")
    ctx_index = lax.axis_index("ctx")
    mp_index = lax.axis_index("mp")
    rep_index = lax.axis_index("rep")
    ids = jnp.stack([mp_index, rep_index]).astype(jnp.int32)
    pages, page, width = token_pages.shape
    rows = pages * page
    cols = decay_floor.shape[0]
    kwide = width // 4
    full, _ = feed_sizes(trainer_gate_up.shape[2])

    packed_mixer = pack_mixer(ids, trainer_mixer_in, trainer_mixer_out)
    plane_mixer = across_plane(packed_mixer, mp_index)
    w_mixer = along_line(plane_mixer, ctx_index, ctx_count).reshape(width, 4 * cols)

    packed_feed = pack_feed(ids, trainer_gate_up, trainer_down)
    plane_feed = across_plane(packed_feed, mp_index)
    w_feed = lax.all_gather(plane_feed, "ctx", axis=0, tiled=True).reshape(4, kwide, -1)

    page_live = live_flags * page
    live_total = jnp.broadcast_to(jnp.sum(page_live), (8, 128)).astype(jnp.int32)
    base = sum(part[0, 0] for part in from_earlier(live_total, ctx_count))
    page_start = base + jnp.cumsum(page_live) - page_live
    positions = (page_start[:, None] + jnp.arange(page, dtype=jnp.int32)[None, :]).reshape(rows)
    starts = jnp.cumsum(lengths) - lengths
    live_tokens = jnp.repeat(live_flags, page)
    resets = (live_tokens == 1) & jnp.any(positions[:, None] == starts[None, :], axis=1)
    count = jnp.cumsum(resets.astype(jnp.int32))
    cnt_col = count.reshape(rows, 1)
    cnt_row = count.reshape(pages, 1, page)
    last = count.reshape(pages, page)[:, -1]

    normed = normalise(page_table, token_pages, mixer_gain)
    half_pages = pages // 2
    table_half = lax.dynamic_slice_in_dim(page_table, rep_index * half_pages, half_pages, 0)
    token_cols = lax.dynamic_slice_in_dim(token_pages, mp_index * kwide, kwide, 2)
    ordered = jnp.take(token_cols, table_half, axis=0).reshape(rows // 2, kwide)

    qs, ks, v, fin, pack = project(
        live_flags, last, normed, w_mixer, decay_floor.reshape(1, cols), cnt_col
    )
    earlier = from_earlier(pack, ctx_count)
    terms = mix(
        last, ids, earlier, qs, ks, v, fin, w_mixer.reshape(4, kwide, 4 * cols), cnt_col, cnt_row
    )
    residual = ordered.astype(F32) + sum_scatter(terms)
    mine, other = gather_plane(residual.astype(BF))
    down_terms = feed_forward(ids, mine, other, feed_gain.reshape(4, 1, kwide), w_feed, full)
    summed = residual + sum_scatter(down_terms)
    live_half = lax.dynamic_slice_in_dim(live_tokens, rep_index * (rows // 2), rows // 2, 0)
    return jnp.where(live_half[:, None] == 1, summed, 0.0).astype(BF)


def solution(mesh):
    in_specs = (
        P("ctx", None, None),
        P("ctx"),
        P("ctx"),
        P(),
        P(("mp", "rep")),
        P(),
        P(),
        P(None, ("ctx", "mp"), None),
        P(None, ("ctx", "mp")),
        P(None, ("ctx", "mp"), None),
        P(None, ("ctx", "mp")),
    )
    out_specs = P(("ctx", "rep"), "mp")
    return jax.shard_map(shards, mesh=mesh, in_specs=in_specs, out_specs=out_specs, check_vma=False)
```

```python
import functools

import jax
import jax.numpy as jnp
from jax import lax
from jax.experimental import pallas as pl
from jax.experimental.pallas import tpu as pltpu
from jax.sharding import PartitionSpec as P

HEAD = 128
EPS = 1e-05
BF = jnp.bfloat16
F32 = jnp.float32
VMEM_LIMIT = 48 * 1024 * 1024
FAR_TILES = 2


def nt(a, b):
    return lax.dot_general(a, b, (((1,), (1,)), ((), ())), preferred_element_type=F32)


def tn(a, b):
    return lax.dot_general(a, b, (((0,), (0,)), ((), ())), preferred_element_type=F32)


def nn(a, b):
    return jnp.dot(a, b, preferred_element_type=F32)


def sigmoid(v):
    return 1.0 / (1.0 + jnp.exp(-v))


def call(body, grid, in_specs, out_specs, out_shape, scratch=(), prefetch=1, cost=None):
    return pl.pallas_call(
        body,
        out_shape=out_shape,
        grid_spec=pltpu.PrefetchScalarGridSpec(
            num_scalar_prefetch=prefetch,
            grid=grid,
            in_specs=in_specs,
            out_specs=out_specs,
            scratch_shapes=list(scratch),
        ),
        compiler_params=pltpu.CompilerParams(
            dimension_semantics=("arbitrary",) * len(grid), vmem_limit_bytes=VMEM_LIMIT
        ),
        cost_estimate=None
        if cost is None
        else pl.CostEstimate(flops=cost[0], bytes_accessed=cost[1], transcendentals=0),
    )


def whole(shape):
    zeros = (0,) * len(shape)
    return pl.BlockSpec(shape, lambda *_: zeros, pipeline_mode=pl.Buffered(1))


def place(shape, index):
    return pl.BlockSpec(shape, lambda *_: (index, 0, 0), pipeline_mode=pl.Buffered(1))


def pack_mixer(ids, mixer_in, mixer_out):
    width = mixer_in.shape[1]
    cols = mixer_in.shape[2] // 8

    def body(ids_ref, q_ref, f_ref, v_ref, o_ref, in_ref, out_ref):
        in_ref[0, :, 0:cols] = q_ref[0].astype(BF)
        in_ref[0, :, cols : 2 * cols] = f_ref[0].astype(BF)
        in_ref[0, :, 2 * cols : 3 * cols] = v_ref[0].astype(BF)
        out_ref[0] = o_ref[...].T.astype(BF)

    def dest(s, ids_ref):
        return 2 * (ids_ref[0] ^ s) + ids_ref[1]

    def part(i):
        return pl.BlockSpec((1, width, cols), lambda s, r: (i, 0, dest(s, r)))

    return call(
        body,
        (4,),
        [part(0), part(1), part(2), pl.BlockSpec((cols, width), lambda s, r: (dest(s, r), 0))],
        [
            pl.BlockSpec((1, width, 3 * cols), lambda s, r: (s, 0, 0)),
            pl.BlockSpec((1, width, cols), lambda s, r: (s, 0, 0)),
        ],
        [
            jax.ShapeDtypeStruct((4, width, 3 * cols), BF),
            jax.ShapeDtypeStruct((4, width, cols), BF),
        ],
        cost=(0, 4 * width * cols * 24),
    )(ids, mixer_in, mixer_in, mixer_in, mixer_out)


class Feed:
    def __init__(self, hidden_all, far):
        tiles = hidden_all // 128 // 8
        self.half_at = 8 * tiles
        assert hidden_all == (8 * tiles + 4) * 128
        self.far, self.near = far * 128, (tiles - far) * 128
        self.near_up = 2 * self.near + 128
        self.near_all = self.near_up + self.near + 128
        self.far_all = 3 * self.far


def pack_feed(ids, gate_up, down, feed):
    width = gate_up.shape[1]
    near, far, up, both = feed.near, feed.far, feed.near_up, feed.near_all
    total = both + feed.far_all

    def body(ids_ref, *refs):
        g_ref, u_ref, gh_ref, uh_ref, d_ref, dh_ref = refs[:6]
        out_ref = refs[-1]
        odd = (ids_ref[0] ^ pl.program_id(0)) % 2
        out_ref[0, :, 0:near] = g_ref[0].astype(BF)
        lane = lax.broadcasted_iota(jnp.int32, (width, 128), 1)
        gh, uh = gh_ref[0], uh_ref[0]
        even_mix = jnp.where(lane < 64, gh, pltpu.roll(uh, 64, 1))
        odd_mix = jnp.where(lane < 64, pltpu.roll(gh, 64, 1), uh)
        out_ref[0, :, near : near + 128] = jnp.where(odd == 1, odd_mix, even_mix).astype(BF)
        out_ref[0, :, near + 128 : up] = u_ref[0].astype(BF)
        out_ref[0, :, up : up + near] = d_ref[...].T.astype(BF)
        last = jnp.concatenate([dh_ref[...], jnp.zeros((64, width), F32)], axis=0)
        out_ref[0, :, up + near : both] = last.T.astype(BF)
        if far:
            fg_ref, fu_ref, fd_ref = refs[6:9]
            out_ref[0, :, both : both + far] = fg_ref[0].astype(BF)
            out_ref[0, :, both + far : both + 2 * far] = fu_ref[0].astype(BF)
            out_ref[0, :, both + 2 * far : total] = fd_ref[...].T.astype(BF)

    def dest(s, r):
        return 4 * r[1] + (r[0] ^ s)

    def tile(s, r):
        return feed.half_at + 2 * r[1] + (r[0] ^ s) // 2

    skip = 8 * near // far if far else 0
    assert skip * far == (8 * near if far else 0)

    def cols(i):
        return pl.BlockSpec((1, width, near), lambda s, r: (i, 0, dest(s, r)))

    def mix(i):
        return pl.BlockSpec((1, width, 128), lambda s, r: (i, 0, tile(s, r)))

    in_specs = [
        cols(0),
        cols(1),
        mix(0),
        mix(1),
        pl.BlockSpec((near, width), lambda s, r: (dest(s, r), 0)),
        pl.BlockSpec((64, width), lambda s, r: (2 * feed.half_at + dest(s, r), 0)),
    ]
    args = [gate_up, gate_up, gate_up, gate_up, down, down]
    if far:
        in_specs += [
            pl.BlockSpec((1, width, far), lambda s, r: (0, 0, skip + dest(s, r))),
            pl.BlockSpec((1, width, far), lambda s, r: (1, 0, skip + dest(s, r))),
            pl.BlockSpec((far, width), lambda s, r: (skip + dest(s, r), 0)),
        ]
        args += [gate_up, gate_up, down]
    return call(
        body,
        (4,),
        in_specs,
        pl.BlockSpec((1, width, total), lambda s, r: (s, 0, 0)),
        jax.ShapeDtypeStruct((4, width, total), BF),
        cost=(0, 4 * width * total * 6),
    )(ids, *args)


def mp_perm(value, s):
    return lax.ppermute(value, "mp", [(i, i ^ s) for i in range(4)])


def rep_perm(value):
    return lax.ppermute(value, "rep", [(0, 1), (1, 0)])


def across_plane(packed, mp_index, cuts):
    arrived = [packed[0]] + [mp_perm(packed[s], s) for s in (1, 2, 3)]
    outs = []
    for low, high in zip(cuts[:-1], cuts[1:]):
        out = jnp.zeros((4, packed.shape[1], high - low), packed.dtype)
        for s in range(4):
            out = lax.dynamic_update_index_in_dim(out, arrived[s][:, low:high], mp_index ^ s, 0)
        outs.append(out.reshape(4 * packed.shape[1], high - low))
    return outs, arrived[1:]


def along_line(block, ctx_index, count):
    out = jnp.zeros((3 * count - 2, *block.shape), block.dtype)
    out = lax.dynamic_update_index_in_dim(out, block, ctx_index + count - 1, 0)
    low = high = block
    steps = []
    for d in range(1, count):
        low = lax.ppermute(low, "ctx", [(i, i + 1) for i in range(count - 1)])
        high = lax.ppermute(high, "ctx", [(i + 1, i) for i in range(count - 1)])
        steps.append((low, high))
        out = lax.dynamic_update_index_in_dim(out, low, ctx_index - d + count - 1, 0)
        out = lax.dynamic_update_index_in_dim(out, high, ctx_index + d + count - 1, 0)
    return out, steps


def after(value, *others):
    return lax.optimization_barrier((value, *others))[0]


def from_earlier(value, count):
    return [
        lax.ppermute(value, "ctx", [(i, i + d) for i in range(count - d)]) for d in range(1, count)
    ]


def normalise(page_table, token_pages, gain):
    pages, page, width = token_pages.shape

    def body(table_ref, x_ref, g_ref, out_ref):
        x = x_ref[0].astype(F32)
        scale = lax.rsqrt(jnp.mean(x * x, axis=-1, keepdims=True) + EPS)
        out_ref[...] = (x * scale * g_ref[...]).astype(BF)

    return call(
        body,
        (pages,),
        [pl.BlockSpec((1, page, width), lambda i, t: (t[i], 0, 0)), whole((1, width))],
        pl.BlockSpec((page, width), lambda i, t: (i, 0)),
        jax.ShapeDtypeStruct((pages * page, width), BF),
        cost=(pages * page * width * 4, pages * page * width * 4),
    )(page_table, token_pages, gain.reshape(1, width))


def step_state(state, ks, v, same_last, keep, final):
    update = tn(v, jnp.where(same_last, ks, jnp.zeros_like(ks)))
    return (jnp.where(keep, state, 0.0) + update) * final


def project(live, last, normed, weights, first, floor, cnt_col):
    rows, width = normed.shape
    cols = floor.shape[1]
    heads = cols // HEAD
    pages = live.shape[0]
    page = rows // pages
    group = 2
    steps = pages // group
    deep = width // 4

    def body(live_ref, last_ref, x_ref, *refs):
        w_refs = refs[:4]
        fl_ref, cnt_ref, qs_ref, ks_ref, v_ref, fin_ref, st_ref, state, total = refs[4:]
        step = pl.program_id(0)

        @pl.when(step == 0)
        def _():
            state[...] = jnp.zeros_like(state)
            total[...] = jnp.zeros_like(total)

        proj = None
        for k in range(4):
            term = nn(x_ref[:, k * deep : (k + 1) * deep], w_refs[k][0])
            proj = term if proj is None else proj + term
        row = lax.broadcasted_iota(jnp.int32, (page, page), 0)
        col = lax.broadcasted_iota(jnp.int32, (page, page), 1)
        lower = (row >= col).astype(F32)
        floor_row = fl_ref[...]
        for j in range(group):
            p = step * group + j
            here = slice(j * page, (j + 1) * page)
            alive = live_ref[p].astype(F32)
            now = last_ref[p]
            before = jnp.where(p == 0, 0, last_ref[jnp.maximum(p - 1, 0)])
            q = proj[here, 0:cols]
            q = q * sigmoid(q)
            f = proj[here, cols : 2 * cols]
            gate = sigmoid(f)
            forget = floor_row + (1.0 - floor_row) * gate
            key = (1.0 - forget) * alive
            log_decay = jnp.log(forget) * alive
            cum = jnp.dot(lower, log_decay, precision=lax.Precision.HIGHEST, preferred_element_type=F32)
            final_log = cum[page - 1 : page, :]
            final = jnp.exp(final_log)
            ks = (key * jnp.exp(-cum)).astype(BF)
            v = proj[here, 2 * cols : 3 * cols].astype(BF)
            qs_ref[here, :] = (q * jnp.exp(cum)).astype(BF)
            ks_ref[here, :] = ks
            v_ref[here, :] = v
            fin_ref[j] = final
            total[...] += final_log
            same_last = cnt_ref[here, :] == now
            for h in range(heads):
                hc = slice(h * HEAD, (h + 1) * HEAD)
                state[h] = step_state(state[h], ks[:, hc], v[:, hc], same_last, now == before, final[:, hc])

        @pl.when(step == steps - 1)
        def _():
            none = last_ref[pages - 1] == 0
            decay = jnp.where(none, jnp.exp(total[...]), 0.0)
            for h in range(heads):
                st_ref[h, 0:HEAD, :] = state[h].astype(BF)
                st_ref[h, HEAD : HEAD + 16, :] = jnp.broadcast_to(
                    decay[:, h * HEAD : (h + 1) * HEAD], (16, HEAD)
                ).astype(BF)

    block = group * page
    return call(
        body,
        (steps,),
        [
            pl.BlockSpec((block, width), lambda i, *_: (i, 0)),
        ]
        + [place((1, deep, 3 * cols), first + k) for k in range(4)]
        + [
            whole((1, cols)),
            pl.BlockSpec((block, 1), lambda i, *_: (i, 0)),
        ],
        [
            pl.BlockSpec((block, cols), lambda i, *_: (i, 0)),
            pl.BlockSpec((block, cols), lambda i, *_: (i, 0)),
            pl.BlockSpec((block, cols), lambda i, *_: (i, 0)),
            pl.BlockSpec((group, 1, cols), lambda i, *_: (i, 0, 0)),
            whole((heads, HEAD + 16, HEAD)),
        ],
        [
            jax.ShapeDtypeStruct((rows, cols), BF),
            jax.ShapeDtypeStruct((rows, cols), BF),
            jax.ShapeDtypeStruct((rows, cols), BF),
            jax.ShapeDtypeStruct((pages, 1, cols), F32),
            jax.ShapeDtypeStruct((heads, HEAD + 16, HEAD), BF),
        ],
        scratch=[pltpu.VMEM((heads, HEAD, HEAD), F32), pltpu.VMEM((1, cols), F32)],
        prefetch=2,
        cost=(2 * rows * width * 3 * cols, rows * width * 2 + width * cols * 8),
    )(live, last, normed, *[weights] * 4, floor, cnt_col)


def mix(last, ids, earlier, qs, ks, v, fin, weights, first, cnt_col, cnt_row):
    rows, cols = qs.shape
    heads = cols // HEAD
    pages = fin.shape[0]
    page = rows // pages
    group = 2
    steps = pages // group
    width = weights.shape[1] * 4
    n = len(earlier)

    def body(last_ref, ids_ref, *refs):
        packs = refs[:n]
        qs_ref, ks_ref, v_ref, fin_ref = refs[n : n + 4]
        w_refs = refs[n + 4 : n + 8]
        cc_ref, cr_ref, out_ref, state = refs[n + 8 :]
        step = pl.program_id(0)

        @pl.when(step == 0)
        def _():
            for h in range(heads):
                total = jnp.zeros((HEAD, HEAD), F32)
                for pack in reversed(packs):
                    total = total * pack[h, HEAD : HEAD + 1, :].astype(F32) + pack[h, 0:HEAD, :].astype(F32)
                state[h] = total

        row = lax.broadcasted_iota(jnp.int32, (page, page), 0)
        col = lax.broadcasted_iota(jnp.int32, (page, page), 1)
        lower = row >= col
        normed = []
        for j in range(group):
            p = step * group + j
            here = slice(j * page, (j + 1) * page)
            now = last_ref[p]
            before = jnp.where(p == 0, 0, last_ref[jnp.maximum(p - 1, 0)])
            cc, cr = cc_ref[here, :], cr_ref[j]
            allowed = lower & (cc == cr)
            reached = cc == before
            same_last = cc == now
            for h in range(heads):
                hc = slice(h * HEAD, (h + 1) * HEAD)
                q_h, k_h, v_h = qs_ref[here, hc], ks_ref[here, hc], v_ref[here, hc]
                scores = jnp.where(allowed, nt(q_h, k_h), 0.0).astype(BF)
                out = nn(scores, v_h)
                out = out + jnp.where(reached, nt(q_h, state[h].astype(BF)), 0.0)
                state[h] = step_state(state[h], k_h, v_h, same_last, now == before, fin_ref[j, :, hc])
                scale = lax.rsqrt(jnp.mean(out * out, axis=-1, keepdims=True) + EPS)
                normed.append((out * scale).astype(BF))
        hn = jnp.concatenate(
            [jnp.concatenate(normed[j * heads : (j + 1) * heads], axis=1) for j in range(group)], axis=0
        )
        for dc in range(2):
            for dy in range(2):
                out_ref[dc, 0, 0, dy] = nt(hn, w_refs[2 * dy + dc][0]).astype(BF)

    block = group * page
    rowspec = pl.BlockSpec((block, cols), lambda i, *_: (i, 0))

    def by_mp(d):
        return pl.BlockSpec(
            (1, *weights.shape[1:]),
            lambda i, l, r: (first + (r[0] ^ d), 0, 0),
            pipeline_mode=pl.Buffered(1),
        )

    return call(
        body,
        (steps,),
        [whole(e.shape) for e in earlier]
        + [
            rowspec,
            rowspec,
            rowspec,
            pl.BlockSpec((group, 1, cols), lambda i, *_: (i, 0, 0)),
        ]
        + [by_mp(d) for d in range(4)]
        + [
            pl.BlockSpec((block, 1), lambda i, *_: (i, 0)),
            pl.BlockSpec((group, 1, page), lambda i, *_: (i, 0, 0)),
        ],
        pl.BlockSpec(
            (2, 1, 1, 2, block, width // 4), lambda i, l, r: (0, i % 2, (i // 2) ^ r[1], 0, 0, 0)
        ),
        jax.ShapeDtypeStruct((2, 2, 2, 2, block, width // 4), BF),
        scratch=[pltpu.VMEM((heads, HEAD, HEAD), F32)],
        prefetch=2,
        cost=(2 * rows * cols * width, rows * width * 2),
    )(last, ids, *earlier, qs, ks, v, fin, *[weights] * 4, cnt_col, cnt_row)


def add(a, b):
    return (a.astype(F32) + b.astype(F32)).astype(BF)


def sum_scatter(terms):
    total = add(terms[0], mp_perm(terms[1], 1))
    a_first = add(total[0, 0], rep_perm(total[0, 1]))
    b_first = add(total[1, :, 0], mp_perm(total[1, :, 1], 2))
    a = a_first[0].astype(F32) + mp_perm(a_first[1], 2).astype(F32)
    b = b_first[0].astype(F32) + rep_perm(b_first[1]).astype(F32)
    return jnp.concatenate([a, b], axis=0)


def gather_plane(value):
    half = value.shape[0] // 2
    a, b = value[:half], value[half:]
    a_y, b_x = mp_perm(a, 2), rep_perm(b)
    a_pair, b_pair = jnp.stack([a, a_y]), jnp.stack([b, b_x])
    a_x, b_y = rep_perm(a_pair), mp_perm(b_pair, 2)
    mine = jnp.stack([jnp.stack([a_pair, a_x]), jnp.stack([b_pair, b_y], axis=1)])
    return mine, mp_perm(mine, 1)


def feed_inputs(ids_ref, m_ref, o_ref, g_ref):
    mp_index = ids_ref[0]
    places = [(dy, dc) for dy in range(2) for dc in range(2)]
    blocks = [(m_ref, o_ref)[dc][0, 0, dy].astype(F32) for dy, dc in places]
    square = sum(jnp.sum(b * b, axis=-1, keepdims=True) for b in blocks)
    scale = lax.rsqrt(square / (4 * blocks[0].shape[1]) + EPS)
    at = [mp_index ^ (2 * dy + dc) for dy, dc in places]
    return places, at, [(b * scale * g_ref[k]).astype(BF) for k, b in zip(at, blocks)]


def total_of(terms):
    out = None
    for term in terms:
        out = term if out is None else out + term
    return out


def feed_specs(mine, gain):
    rows, kwide = mine.shape[-2:]
    spec = pl.BlockSpec((1, 1, 2, rows, kwide), lambda i, r: (i % 2, i // 2, 0, 0, 0))
    out_spec = pl.BlockSpec((2, 1, 1, 2, rows, kwide), lambda i, r: (0, i % 2, i // 2, 0, 0, 0))
    return [spec, spec, whole(gain.shape)], out_spec, jax.ShapeDtypeStruct((2, 2, 2, 2, rows, kwide), BF)


def feed_near(ids, mine, other, gain, weights, feed, extra=None):
    near, up, both = feed.near, feed.near_up, feed.near_all
    specs, out_spec, out_shape = feed_specs(mine, gain)

    def body(ids_ref, m_ref, o_ref, g_ref, w_ref, *rest):
        out_ref = rest[-1]
        places, at, xs = feed_inputs(ids_ref, m_ref, o_ref, g_ref)
        h = total_of(nn(x, w_ref[k, :, 0:up]) for k, x in zip(at, xs))
        gate, upward = h[:, 0:near], h[:, near + 128 : up]
        edge = h[:, near : near + 128]
        hidden = gate * sigmoid(gate) * upward
        mixed = edge * sigmoid(edge) * pltpu.roll(edge, 64, 1)
        lane = lax.broadcasted_iota(jnp.int32, mixed.shape, 1)
        mixed = jnp.where(lane < 64, mixed, 0.0)
        hidden = jnp.concatenate([hidden, mixed], axis=1).astype(BF)
        for (dy, dc), k in zip(places, at):
            term = nt(hidden, w_ref[k, :, up:both])
            if extra is not None:
                term = term + jnp.where(ids_ref[2] == 1, rest[0][dc, 0, 0, dy].astype(F32), 0.0)
            out_ref[dc, 0, 0, dy] = term.astype(BF)

    rows = out_shape.shape[-2] * 4
    return call(
        body,
        (4,),
        specs + [whole(weights.shape)] + ([] if extra is None else [out_spec]),
        out_spec,
        out_shape,
        cost=(2 * rows * weights.size, weights.size * 2 + 3 * out_shape.size * 2),
    )(ids, mine, other, gain, weights, *([] if extra is None else [extra]))


def feed_far(ids, mine, other, gain, weights, feed):
    far = feed.far
    specs, out_spec, out_shape = feed_specs(mine, gain)

    def body(ids_ref, m_ref, o_ref, g_ref, w_ref, out_ref):
        @pl.when(ids_ref[2] == 1)
        def _():
            places, at, xs = feed_inputs(ids_ref, m_ref, o_ref, g_ref)
            where = [ids_ref[3 + k] for k in at]
            h = total_of(nn(x, w_ref[k, :, 0 : 2 * far]) for k, x in zip(where, xs))
            gate, upward = h[:, 0:far], h[:, far : 2 * far]
            hidden = (gate * sigmoid(gate) * upward).astype(BF)
            for (dy, dc), k in zip(places, where):
                out_ref[dc, 0, 0, dy] = nt(hidden, w_ref[k, :, 2 * far : 3 * far]).astype(BF)

    rows = out_shape.shape[-2] * 4
    return call(
        body,
        (4,),
        specs + [whole(weights.shape)],
        out_spec,
        out_shape,
        cost=(2 * rows * weights.size, weights.size * 2 + 2 * out_shape.size * 2),
    )(ids, mine, other, gain, weights)


def shards(
    token_pages,
    page_table,
    live_flags,
    lengths,
    decay_floor,
    mixer_gain,
    feed_gain,
    trainer_mixer_in,
    trainer_mixer_out,
    trainer_gate_up,
    trainer_down,
):
    ctx_count = lax.axis_size("ctx")
    ctx_index = lax.axis_index("ctx")
    mp_index = lax.axis_index("mp")
    rep_index = lax.axis_index("rep")
    split = ctx_count == 4
    middle = (ctx_index == 1) | (ctx_index == 2)
    beyond = jnp.where(ctx_index == 1, 0, 3)
    order = [
        jnp.where(k == ctx_index, 0, 1) if k in (1, 2) else jnp.where(k == beyond, 2, 3) for k in range(4)
    ]
    ids = jnp.stack([mp_index, rep_index, middle.astype(jnp.int32), *order]).astype(jnp.int32)
    pages, page, width = token_pages.shape
    rows = pages * page
    cols = decay_floor.shape[0]
    kwide = width // 4
    feed = Feed(trainer_gate_up.shape[2], FAR_TILES if split else 0)

    packed_in, packed_out = pack_mixer(ids, trainer_mixer_in, trainer_mixer_out)
    (plane_in,), moved = across_plane(packed_in, mp_index, (0, 3 * cols))
    packed_feed = pack_feed(ids, trainer_gate_up, trainer_down, feed)
    packed_out, packed_feed, *_ = lax.optimization_barrier((packed_out, packed_feed, *moved))
    (plane_out,), _ = across_plane(packed_out, mp_index, (0, cols))
    cuts = (0, feed.near_all, feed.near_all + feed.far_all)
    plane_feed, _ = across_plane(packed_feed, mp_index, cuts if split else cuts[:2])
    if split:
        w_in, steps = along_line(plane_in, ctx_index, ctx_count)
        w_out, _ = along_line(after(plane_out, *steps[2]), ctx_index, ctx_count)
        first = ctx_count - 1
        plane_near, plane_far = plane_feed
        plane_far = after(plane_far, *steps[1])
        across = lax.ppermute(plane_far, "ctx", [(1, 2), (2, 1)])
        inward = lax.ppermute(plane_far, "ctx", [(0, 1), (3, 2)])
        onward = lax.ppermute(inward, "ctx", [(1, 2), (2, 1)])
        w_far = jnp.stack([plane_far, across, inward, onward])
        plane_near = after(plane_near, *steps[1])
    else:
        w_in = lax.all_gather(plane_in, "ctx", axis=0, tiled=True).reshape(4, kwide, -1)
        w_out = lax.all_gather(plane_out, "ctx", axis=0, tiled=True).reshape(4, kwide, -1)
        first = 0
        plane_near = plane_feed[0]
    w_near = lax.all_gather(plane_near, "ctx", axis=0, tiled=True).reshape(4, kwide, -1)

    page_live = live_flags * page
    live_total = jnp.broadcast_to(jnp.sum(page_live), (8, 128)).astype(jnp.int32)
    base = sum(part[0, 0] for part in from_earlier(live_total, ctx_count))
    page_start = base + jnp.cumsum(page_live) - page_live
    positions = (page_start[:, None] + jnp.arange(page, dtype=jnp.int32)[None, :]).reshape(rows)
    starts = jnp.cumsum(lengths) - lengths
    live_tokens = jnp.repeat(live_flags, page)
    resets = (live_tokens == 1) & jnp.any(positions[:, None] == starts[None, :], axis=1)
    count = jnp.cumsum(resets.astype(jnp.int32))
    cnt_col = count.reshape(rows, 1)
    cnt_row = count.reshape(pages, 1, page)
    last = count.reshape(pages, page)[:, -1]

    normed = normalise(page_table, token_pages, mixer_gain)
    half_pages = pages // 2
    table_half = lax.dynamic_slice_in_dim(page_table, rep_index * half_pages, half_pages, 0)
    token_cols = lax.dynamic_slice_in_dim(token_pages, mp_index * kwide, kwide, 2)
    ordered = jnp.take(token_cols, table_half, axis=0).reshape(rows // 2, kwide)

    qs, ks, v, fin, pack = project(
        live_flags, last, normed, w_in, first, decay_floor.reshape(1, cols), cnt_col
    )
    earlier = from_earlier(pack, ctx_count)
    terms = mix(last, ids, earlier, qs, ks, v, fin, w_out, first, cnt_col, cnt_row)
    residual = ordered.astype(F32) + sum_scatter(terms)
    value = residual.astype(BF)
    gain = feed_gain.reshape(4, 1, kwide)
    if split:
        foreign = lax.ppermute(value, "ctx", [(0, 1), (3, 2)])
        mine, other = gather_plane(value)
        extra = feed_far(ids, mine, other, gain, w_far, feed)
        theirs = gather_plane(foreign)
        given = sum_scatter(feed_far(ids, *theirs, gain, w_far, feed))
        back = lax.ppermute(given.astype(BF), "ctx", [(1, 0), (2, 3)])
        down_terms = feed_near(ids, mine, other, gain, w_near, feed, extra)
        summed = residual + sum_scatter(down_terms) + back.astype(F32)
    else:
        mine, other = gather_plane(value)
        summed = residual + sum_scatter(feed_near(ids, mine, other, gain, w_near, feed))
    live_half = lax.dynamic_slice_in_dim(live_tokens, rep_index * (rows // 2), rows // 2, 0)
    return jnp.where(live_half[:, None] == 1, summed, 0.0).astype(BF)


def solution(mesh):
    in_specs = (
        P("ctx", None, None),
        P("ctx"),
        P("ctx"),
        P(),
        P(("mp", "rep")),
        P(),
        P(),
        P(None, ("ctx", "mp"), None),
        P(None, ("ctx", "mp")),
        P(None, ("ctx", "mp"), None),
        P(None, ("ctx", "mp")),
    )
    out_specs = P(("ctx", "rep"), "mp")
    return jax.shard_map(shards, mesh=mesh, in_specs=in_specs, out_specs=out_specs, check_vma=False)
```

```python
import functools

import jax
import jax.numpy as jnp
from jax import lax
from jax.experimental import pallas as pl
from jax.experimental.pallas import tpu as pltpu
from jax.sharding import PartitionSpec as P

HEAD = 128
EPS = 1e-05
BF = jnp.bfloat16
F32 = jnp.float32
VMEM_LIMIT = 48 * 1024 * 1024


def nt(a, b):
    return lax.dot_general(a, b, (((1,), (1,)), ((), ())), preferred_element_type=F32)


def tn(a, b):
    return lax.dot_general(a, b, (((0,), (0,)), ((), ())), preferred_element_type=F32)


def nn(a, b):
    return jnp.dot(a, b, preferred_element_type=F32)


def sigmoid(v):
    return 1.0 / (1.0 + jnp.exp(-v))


def call(body, grid, in_specs, out_specs, out_shape, scratch=(), prefetch=1, cost=None):
    return pl.pallas_call(
        body,
        out_shape=out_shape,
        grid_spec=pltpu.PrefetchScalarGridSpec(
            num_scalar_prefetch=prefetch,
            grid=grid,
            in_specs=in_specs,
            out_specs=out_specs,
            scratch_shapes=list(scratch),
        ),
        compiler_params=pltpu.CompilerParams(
            dimension_semantics=("arbitrary",) * len(grid), vmem_limit_bytes=VMEM_LIMIT
        ),
        cost_estimate=None
        if cost is None
        else pl.CostEstimate(flops=cost[0], bytes_accessed=cost[1], transcendentals=0),
    )


def whole(shape):
    zeros = (0,) * len(shape)
    return pl.BlockSpec(shape, lambda *_: zeros, pipeline_mode=pl.Buffered(1))


ANY = pl.BlockSpec(memory_space=pl.ANY)


class Rows:
    def __init__(self, arrays, low=0, high=None):
        self.arrays = list(arrays)
        self.planes, self.rows, columns = (
            self.arrays[0].shape if len(self.arrays) == 1 else (len(arrays), *self.arrays[0].shape)
        )
        self.part = slice(low, columns if high is None else high)
        self.scratch = [
            pltpu.VMEM((self.planes * self.rows, self.part.stop - low), BF),
            pltpu.SemaphoreType.DMA((self.planes * 4,)),
        ]

    def copies(self, ids_ref, refs, held, sems):
        rows = self.rows // 4
        for i in range(self.planes):
            ref, plane = (refs[0].at[i], i) if len(refs) == 1 else (refs[i], ids_ref[3 + i])
            for s in range(4):
                to = pl.multiple_of((plane * 4 + (ids_ref[0] ^ s)) * rows, rows)
                yield pltpu.make_async_copy(
                    ref.at[pl.ds(s * rows, rows), self.part], held.at[pl.ds(to, rows)], sems.at[4 * i + s]
                )

    def start(self, *where):
        for copy in self.copies(*where):
            copy.start()

    def wait(self, *where):
        for copy in self.copies(*where):
            copy.wait()


def pack_mixer(ids, mixer_in, mixer_out):
    width = mixer_in.shape[1]
    cols = mixer_in.shape[2] // 8

    def body(ids_ref, q_ref, f_ref, v_ref, o_ref, out_ref):
        out_ref[0, :, 0:cols] = q_ref[0].astype(BF)
        out_ref[0, :, cols : 2 * cols] = f_ref[0].astype(BF)
        out_ref[0, :, 2 * cols : 3 * cols] = v_ref[0].astype(BF)
        out_ref[0, :, 3 * cols : 4 * cols] = o_ref[...].T.astype(BF)

    def dest(s, ids_ref):
        return 2 * (ids_ref[0] ^ s) + ids_ref[1]

    def part(i):
        return pl.BlockSpec((1, width, cols), lambda s, r: (i, 0, dest(s, r)))

    return call(
        body,
        (4,),
        [part(0), part(1), part(2), pl.BlockSpec((cols, width), lambda s, r: (dest(s, r), 0))],
        pl.BlockSpec((1, width, 4 * cols), lambda s, r: (s, 0, 0)),
        jax.ShapeDtypeStruct((4, width, 4 * cols), BF),
        cost=(0, 4 * width * cols * 24),
    )(ids, mixer_in, mixer_in, mixer_in, mixer_out)


class Feed:
    def __init__(self, hidden_all):
        tiles = hidden_all // 128 // 8
        self.half_at = 8 * tiles
        assert hidden_all == (8 * tiles + 4) * 128
        self.near = tiles * 128
        self.near_up = 2 * self.near + 128
        self.near_all = self.near_up + self.near + 128


def pack_feed(ids, gate_up, down, feed):
    width = gate_up.shape[1]
    near, up, both = feed.near, feed.near_up, feed.near_all

    def body(ids_ref, *refs):
        g_ref, u_ref, gh_ref, uh_ref, d_ref, dh_ref = refs[:6]
        out_ref = refs[-1]
        odd = (ids_ref[0] ^ pl.program_id(0)) % 2
        out_ref[0, :, 0:near] = g_ref[0].astype(BF)
        lane = lax.broadcasted_iota(jnp.int32, (width, 128), 1)
        gh, uh = gh_ref[0], uh_ref[0]
        even_mix = jnp.where(lane < 64, gh, pltpu.roll(uh, 64, 1))
        odd_mix = jnp.where(lane < 64, pltpu.roll(gh, 64, 1), uh)
        out_ref[0, :, near : near + 128] = jnp.where(odd == 1, odd_mix, even_mix).astype(BF)
        out_ref[0, :, near + 128 : up] = u_ref[0].astype(BF)
        out_ref[0, :, up : up + near] = d_ref[...].T.astype(BF)
        last = jnp.concatenate([dh_ref[...], jnp.zeros((64, width), F32)], axis=0)
        out_ref[0, :, up + near : both] = last.T.astype(BF)

    def dest(s, r):
        return 4 * r[1] + (r[0] ^ s)

    def tile(s, r):
        return feed.half_at + 2 * r[1] + (r[0] ^ s) // 2


    def cols(i):
        return pl.BlockSpec((1, width, near), lambda s, r: (i, 0, dest(s, r)))

    def mix(i):
        return pl.BlockSpec((1, width, 128), lambda s, r: (i, 0, tile(s, r)))

    in_specs = [
        cols(0),
        cols(1),
        mix(0),
        mix(1),
        pl.BlockSpec((near, width), lambda s, r: (dest(s, r), 0)),
        pl.BlockSpec((64, width), lambda s, r: (2 * feed.half_at + dest(s, r), 0)),
    ]
    args = [gate_up, gate_up, gate_up, gate_up, down, down]
    return call(
        body,
        (4,),
        in_specs,
        pl.BlockSpec((1, width, both), lambda s, r: (s, 0, 0)),
        jax.ShapeDtypeStruct((4, width, both), BF),
        cost=(0, 4 * width * both * 6),
    )(ids, *args)


def mp_perm(value, s):
    return lax.ppermute(value, "mp", [(i, i ^ s) for i in range(4)])


def rep_perm(value):
    return lax.ppermute(value, "rep", [(0, 1), (1, 0)])


def across_plane(packed):
    moved = [mp_perm(packed[s], s) for s in (1, 2, 3)]
    return jnp.concatenate([packed[0], *moved], axis=0), moved


def after(value, *others):
    return lax.optimization_barrier((value, *others))[0]


def from_earlier(value, count):
    return [
        lax.ppermute(value, "ctx", [(i, i + d) for i in range(count - d)]) for d in range(1, count)
    ]


def total_before(value, count):
    shift = 1
    total = lax.ppermute(value, "ctx", [(i, i + 1) for i in range(count - 1)])
    so_far = total + value
    while 2 * shift < count:
        came = lax.ppermute(so_far, "ctx", [(i, i + 2 * shift) for i in range(count - 2 * shift)])
        total, so_far, shift = total + came, so_far + came, 2 * shift
    return total


def normalise(table, token_pages, gain):
    _, page, width = token_pages.shape
    pages = table.shape[0]

    def body(table_ref, x_ref, g_ref, out_ref):
        x = x_ref[0].astype(F32)
        scale = lax.rsqrt(jnp.mean(x * x, axis=-1, keepdims=True) + EPS)
        out_ref[...] = (x * scale * g_ref[...]).astype(BF)

    return call(
        body,
        (pages,),
        [pl.BlockSpec((1, page, width), lambda i, t: (t[i], 0, 0)), whole((1, width))],
        pl.BlockSpec((page, width), lambda i, t: (i, 0)),
        jax.ShapeDtypeStruct((pages * page, width), BF),
        cost=(pages * page * width * 4, pages * page * width * 4),
    )(table, token_pages, gain.reshape(1, width))


def step_state(state, ks, v, same_last, keep, final):
    update = tn(v, jnp.where(same_last, ks, jnp.zeros_like(ks)))
    return (jnp.where(keep, state, 0.0) + update) * final


def project(ids, live, last, normed, foreign, weights, floor, cnt_col):
    width = normed.shape[1]
    cols = floor.shape[1]
    heads = cols // HEAD
    pages = live.shape[0]
    rows = cnt_col.shape[0]
    page = rows // pages
    group = 2
    steps = pages // group

    n = len(weights.arrays)

    def body(ids_ref, *refs):
        pl.when(ids_ref[2] == 1)(lambda: work(ids_ref, *refs))

    def work(ids_ref, live_ref, last_ref, x_ref, *refs):
        f_refs, refs = refs[: len(foreign)], refs[len(foreign) :]
        w_refs = refs[:n]
        fl_ref, cnt_ref, qs_ref, ks_ref, v_ref, fin_ref, st_ref, state, total, held, sems = refs[n:]
        step = pl.program_id(0)

        @pl.when(step == 0)
        def _():
            weights.start(ids_ref, w_refs, held, sems)
            state[...] = jnp.zeros_like(state)
            total[...] = jnp.zeros_like(total)
            weights.wait(ids_ref, w_refs, held, sems)

        x = x_ref[...]
        if foreign:
            mine, other = (f[:, 0, 0].reshape(page, width) for f in f_refs)
            low = (ids_ref[0] & 1) == 0
            pair = jnp.concatenate([jnp.where(low, mine, other), jnp.where(low, other, mine)], axis=0)
            x = jnp.where((step >> 2) == ids_ref[8], x, pair)
        proj = nn(x, held[...])
        row = lax.broadcasted_iota(jnp.int32, (page, page), 0)
        col = lax.broadcasted_iota(jnp.int32, (page, page), 1)
        lower = (row >= col).astype(F32)
        floor_row = fl_ref[...]
        for j in range(group):
            p = step * group + j
            here = slice(j * page, (j + 1) * page)
            alive = live_ref[p].astype(F32)
            now = last_ref[p]
            before = jnp.where(p == 0, 0, last_ref[jnp.maximum(p - 1, 0)])
            q = proj[here, 0:cols]
            q = q * sigmoid(q)
            f = proj[here, cols : 2 * cols]
            gate = sigmoid(f)
            forget = floor_row + (1.0 - floor_row) * gate
            key = (1.0 - forget) * alive
            log_decay = jnp.log(forget) * alive
            cum = jnp.dot(lower, log_decay, precision=lax.Precision.HIGHEST, preferred_element_type=F32)
            final_log = cum[page - 1 : page, :]
            final = jnp.exp(final_log)
            ks = (key * jnp.exp(-cum)).astype(BF)
            v = proj[here, 2 * cols : 3 * cols].astype(BF)
            qs_ref[here, :] = (q * jnp.exp(cum)).astype(BF)
            ks_ref[here, :] = ks
            v_ref[here, :] = v
            fin_ref[j] = final
            total[...] += final_log
            same_last = cnt_ref[here, :] == now
            for h in range(heads):
                hc = slice(h * HEAD, (h + 1) * HEAD)
                state[h] = step_state(state[h], ks[:, hc], v[:, hc], same_last, now == before, final[:, hc])

        @pl.when(step == steps - 1)
        def _():
            none = last_ref[pages - 1] == 0
            decay = jnp.where(none, jnp.exp(total[...]), 0.0)
            for h in range(heads):
                st_ref[h, 0:HEAD, :] = state[h].astype(BF)
                st_ref[h, HEAD : HEAD + 16, :] = jnp.broadcast_to(
                    decay[:, h * HEAD : (h + 1) * HEAD], (16, HEAD)
                ).astype(BF)

    block = group * page
    return call(
        body,
        (steps,),
        [
            pl.BlockSpec((block, width), lambda i, *_: (i & 3, 0)),
        ]
        + [
            pl.BlockSpec(
                (2, 1, 1, page // 2, width),
                lambda i, r, *_: (0, ((i >> 1) & 1) ^ r[1], (i & 1) ^ (r[0] >> 1), 0, 0),
            )
        ]
        * len(foreign)
        + [ANY] * n
        + [
            whole((1, cols)),
            pl.BlockSpec((block, 1), lambda i, *_: (i, 0)),
        ],
        [
            pl.BlockSpec((block, cols), lambda i, *_: (i, 0)),
            pl.BlockSpec((block, cols), lambda i, *_: (i, 0)),
            pl.BlockSpec((block, cols), lambda i, *_: (i, 0)),
            pl.BlockSpec((group, 1, cols), lambda i, *_: (i, 0, 0)),
            whole((heads, HEAD + 16, HEAD)),
        ],
        [
            jax.ShapeDtypeStruct((rows, cols), BF),
            jax.ShapeDtypeStruct((rows, cols), BF),
            jax.ShapeDtypeStruct((rows, cols), BF),
            jax.ShapeDtypeStruct((pages, 1, cols), F32),
            jax.ShapeDtypeStruct((heads, HEAD + 16, HEAD), BF),
        ],
        scratch=[pltpu.VMEM((heads, HEAD, HEAD), F32), pltpu.VMEM((1, cols), F32), *weights.scratch],
        prefetch=3,
        cost=(2 * rows * width * 3 * cols, rows * width * 2 + width * cols * 8),
    )(ids, live, last, normed, *foreign, *weights.arrays, floor, cnt_col)


def mix(ids, last, earlier, qs, ks, v, fin, weights, cnt_col, cnt_row):
    rows, cols = qs.shape
    heads = cols // HEAD
    pages = fin.shape[0]
    page = rows // pages
    group = 2
    steps = pages // group
    width = weights.planes * weights.rows
    n = len(earlier)
    spans = steps // 4
    m = n + 4 + len(weights.arrays)

    def body(ids_ref, *refs):
        pl.when(ids_ref[2] == 1)(lambda: work(ids_ref, *refs))

    def work(ids_ref, last_ref, *refs):
        packs = refs[:n]
        qs_ref, ks_ref, v_ref, fin_ref = refs[n : n + 4]
        w_refs = refs[n + 4 : m]
        cc_ref, cr_ref = refs[m : m + 2]
        outs = refs[m + 2 : m + 2 + 2 * spans]
        state, held, sems = refs[m + 2 + 2 * spans :]
        step = pl.program_id(0)

        @pl.when(step == 0)
        def _():
            weights.start(ids_ref, w_refs, held, sems)
            for h in range(heads):
                total = jnp.zeros((HEAD, HEAD), F32)
                for pack in reversed(packs):
                    total = total * pack[h, HEAD : HEAD + 1, :].astype(F32) + pack[h, 0:HEAD, :].astype(F32)
                state[h] = total

        row = lax.broadcasted_iota(jnp.int32, (page, page), 0)
        col = lax.broadcasted_iota(jnp.int32, (page, page), 1)
        lower = row >= col
        normed = []
        for j in range(group):
            p = step * group + j
            here = slice(j * page, (j + 1) * page)
            now = last_ref[p]
            before = jnp.where(p == 0, 0, last_ref[jnp.maximum(p - 1, 0)])
            cc, cr = cc_ref[here, :], cr_ref[j]
            allowed = lower & (cc == cr)
            reached = cc == before
            same_last = cc == now
            for h in range(heads):
                hc = slice(h * HEAD, (h + 1) * HEAD)
                q_h, k_h, v_h = qs_ref[here, hc], ks_ref[here, hc], v_ref[here, hc]
                scores = jnp.where(allowed, nt(q_h, k_h), 0.0).astype(BF)
                out = nn(scores, v_h)
                out = out + jnp.where(reached, nt(q_h, state[h].astype(BF)), 0.0)
                state[h] = step_state(state[h], k_h, v_h, same_last, now == before, fin_ref[j, :, hc])
                scale = lax.rsqrt(jnp.mean(out * out, axis=-1, keepdims=True) + EPS)
                normed.append((out * scale).astype(BF))
        hn = jnp.concatenate(
            [jnp.concatenate(normed[j * heads : (j + 1) * heads], axis=1) for j in range(group)], axis=0
        )

        @pl.when(step == 0)
        def _():
            weights.wait(ids_ref, w_refs, held, sems)

        for dc in range(2):
            for dy in range(2):
                term = nt(hn, held[block_of(ids_ref[0] ^ (2 * dy + dc), width // 4), :]).astype(BF)
                for span in range(spans):

                    @pl.when((step // 4) ^ ids_ref[8] == span)
                    def _(span=span, dc=dc, dy=dy, term=term):
                        outs[2 * span + dc][0, 0, dy] = term

    block = group * page
    rowspec = pl.BlockSpec((block, cols), lambda i, *_: (i, 0))

    def terms(span):
        def index(i, r, l):
            low = 4 * (span ^ r[8])
            i = jnp.minimum(jnp.maximum(i, low), low + 3) & 3
            return (i % 2, (i // 2) ^ r[1], 0, 0, 0)

        return pl.BlockSpec((1, 1, 2, block, width // 4), index)

    return call(
        body,
        (steps,),
        [whole(e.shape) for e in earlier]
        + [
            rowspec,
            rowspec,
            rowspec,
            pl.BlockSpec((group, 1, cols), lambda i, *_: (i, 0, 0)),
        ]
        + [ANY] * len(weights.arrays)
        + [
            pl.BlockSpec((block, 1), lambda i, *_: (i, 0)),
            pl.BlockSpec((group, 1, page), lambda i, *_: (i, 0, 0)),
        ],
        [terms(span) for span in range(spans) for _ in range(2)],
        [jax.ShapeDtypeStruct((2, 2, 2, block, width // 4), BF)] * (2 * spans),
        scratch=[pltpu.VMEM((heads, HEAD, HEAD), F32), *weights.scratch],
        prefetch=2,
        cost=(2 * rows * cols * width, rows * width * 2),
    )(ids, last, *earlier, qs, ks, v, fin, *weights.arrays, cnt_col, cnt_row)


def add(a, b):
    return (a.astype(F32) + b.astype(F32)).astype(BF)


def sum_scatter(terms):
    mine, other = terms[0], mp_perm(terms[1], 1)
    a_keep, a_send = add(mine[0, 0], other[0, 0]), add(mine[0, 1], other[0, 1])
    b_keep, b_send = add(mine[1, :, 0], other[1, :, 0]), add(mine[1, :, 1], other[1, :, 1])
    a_came, b_came = rep_perm(a_send), mp_perm(b_send, 2)
    a_send, b_send = add(a_keep[1], a_came[1]), add(b_keep[1], b_came[1])
    a_last, b_last = mp_perm(a_send, 2), rep_perm(b_send)
    a = a_keep[0].astype(F32) + a_came[0].astype(F32) + a_last.astype(F32)
    b = b_keep[0].astype(F32) + b_came[0].astype(F32) + b_last.astype(F32)
    return jnp.concatenate([a, b], axis=0), (a_came, b_came)


def gather_plane(value, *others):
    half = value.shape[0] // 2
    a, b = value[:half], value[half:]
    a_y, b_x = mp_perm(a, 2), rep_perm(b)
    a_pair, b_pair = jnp.stack([a, a_y]), jnp.stack([b, b_x])
    a_x, b_y = rep_perm(a_pair), mp_perm(b_pair, 2)
    mine = jnp.stack([jnp.stack([a_pair, a_x]), jnp.stack([b_pair, b_y], axis=1)])
    mine = after(mine, *others)
    return mine, mp_perm(mine, 1)


def feed_inputs(ids_ref, m_ref, o_ref, g_ref):
    mp_index = ids_ref[0]
    places = [(dy, dc) for dy in range(2) for dc in range(2)]
    blocks = [(m_ref, o_ref)[dc][0, 0, dy].astype(F32) for dy, dc in places]
    square = sum(jnp.sum(b * b, axis=-1, keepdims=True) for b in blocks)
    scale = lax.rsqrt(square / (4 * blocks[0].shape[1]) + EPS)
    at = [mp_index ^ (2 * dy + dc) for dy, dc in places]
    return places, at, [(b * scale * g_ref[k]).astype(BF) for k, b in zip(at, blocks)]


def block_of(k, rows):
    return pl.ds(pl.multiple_of(k * rows, rows), rows)


def total_of(terms):
    out = None
    for term in terms:
        out = term if out is None else out + term
    return out


def feed_specs(mine, gain):
    rows, kwide = mine.shape[-2:]
    spec = pl.BlockSpec((1, 1, 2, rows, kwide), lambda i, r: (i % 2, i // 2, 0, 0, 0))
    return [spec, spec, whole(gain.shape)], [spec, spec], [jax.ShapeDtypeStruct((2, 2, 2, rows, kwide), BF)] * 2


def feed_forward(ids, mine, other, gain, weights, feed):
    near, up, both = feed.near, feed.near_up, feed.near_all
    specs, out_spec, out_shape = feed_specs(mine, gain)

    n = len(weights.arrays)

    def body(ids_ref, m_ref, o_ref, g_ref, *rest):
        w_refs, outs, (held, sems) = rest[:n], rest[n : n + 2], rest[n + 2 :]
        first = pl.program_id(0) == 0
        pl.when(first)(lambda: weights.start(ids_ref, w_refs, held, sems))
        places, at, xs = feed_inputs(ids_ref, m_ref, o_ref, g_ref)
        pl.when(first)(lambda: weights.wait(ids_ref, w_refs, held, sems))

        h = total_of(nn(x, held[block_of(k, kwide), 0:up]) for k, x in zip(at, xs))
        gate, upward = h[:, 0:near], h[:, near + 128 : up]
        edge = h[:, near : near + 128]
        hidden = gate * sigmoid(gate) * upward
        mixed = edge * sigmoid(edge) * pltpu.roll(edge, 64, 1)
        lane = lax.broadcasted_iota(jnp.int32, mixed.shape, 1)
        mixed = jnp.where(lane < 64, mixed, 0.0)
        hidden = jnp.concatenate([hidden, mixed], axis=1).astype(BF)
        for (dy, dc), k in zip(places, at):
            term = nt(hidden, held[block_of(k, kwide), up:both])
            outs[dc][0, 0, dy] = term.astype(BF)

    rows, kwide = out_shape[0].shape[-2] * 4, out_shape[0].shape[-1]
    return call(
        body,
        (4,),
        specs + [ANY] * n,
        out_spec,
        out_shape,
        scratch=weights.scratch,
        cost=(rows * 4 * kwide * both * 2, 4 * kwide * both * 2 + 6 * out_shape[0].size * 2),
    )(ids, mine, other, gain, *weights.arrays)


def shards(
    token_pages,
    page_table,
    live_flags,
    lengths,
    decay_floor,
    mixer_gain,
    feed_gain,
    trainer_mixer_in,
    trainer_mixer_out,
    trainer_gate_up,
    trainer_down,
):
    ctx_count = lax.axis_size("ctx")
    ctx_index = lax.axis_index("ctx")
    mp_index = lax.axis_index("mp")
    rep_index = lax.axis_index("rep")
    pages, page, width = token_pages.shape
    cols = decay_floor.shape[0]
    kwide = width // 4
    feed = Feed(trainer_gate_up.shape[2])
    line = ctx_count == 4 and pages == 8
    middle = (ctx_index == 1) | (ctx_index == 2)
    beyond = jnp.where(ctx_index == 1, 0, 3)
    order = [ctx_index, 3 - ctx_index, beyond, 3 - beyond]
    own_span = (ctx_index == 1).astype(jnp.int32) if line else 0
    active = middle.astype(jnp.int32) if line else 1
    ids = jnp.stack([mp_index, rep_index, active, *order, ctx_index, own_span]).astype(jnp.int32)

    def gather(value):
        return Rows([lax.all_gather(value, "ctx", axis=0)])

    if line:
        sent = lax.dynamic_slice_in_dim(page_table, rep_index * 4 + mp_index, 1, 0)
        chunk = normalise(sent, token_pages, mixer_gain)
        ids_next = after(ids, chunk)
        chunk = lax.ppermute(chunk, "ctx", [(0, 1), (3, 2)])
    else:
        ids_next = ids
    packed_mixer = pack_mixer(ids_next, trainer_mixer_in, trainer_mixer_out)
    plane_mixer, moved = across_plane(packed_mixer)
    packed_feed = after(pack_feed(after(ids, packed_mixer), trainer_gate_up, trainer_down, feed), *moved)
    plane_feed, _ = across_plane(packed_feed)
    flags = after(live_flags, packed_mixer)
    if line:
        spread = jnp.broadcast_to(flags[:, None], (pages, 128)).astype(jnp.int32)
        came = lax.ppermute(spread, "ctx", [(0, 1), (3, 2)])
        totals = jnp.broadcast_to(jnp.sum(spread + came, axis=0, keepdims=True), (8, 128))
        base = lax.ppermute(totals, "ctx", [(1, 2)])[0, 0]
        theirs = came[:, 0]
        live_here = jnp.concatenate(
            [jnp.where(ctx_index == 1, theirs, flags), jnp.where(ctx_index == 1, flags, theirs)]
        )
        page_start = (base + jnp.cumsum(live_here) - live_here) * page

        across = lax.ppermute(plane_mixer, "ctx", [(1, 2), (2, 1)])
        inward = lax.ppermute(plane_mixer, "ctx", [(0, 1), (3, 2)])
        onward = lax.ppermute(inward, "ctx", [(1, 2), (2, 1)])
        mixer_rows = [plane_mixer, across, inward, onward]
        plane_feed = after(plane_feed, onward)
        normed = normalise(after(page_table, *moved), token_pages, mixer_gain)
        foreign = gather_plane(chunk, across, inward, normed)
    else:
        normed = normalise(page_table, token_pages, mixer_gain)
        foreign = ()
        live_here = flags
        live_total = jnp.broadcast_to(jnp.sum(flags) * page, (8, 128)).astype(jnp.int32)
        page_start = total_before(live_total, ctx_count)[0, 0] + (jnp.cumsum(flags) - flags) * page
        mixer_rows = gather(plane_mixer).arrays
    w_feed = gather(plane_feed)

    rows = live_here.shape[0] * page
    positions = (page_start[:, None] + jnp.arange(page, dtype=jnp.int32)[None, :]).reshape(rows)
    starts = jnp.cumsum(lengths) - lengths
    resets = (jnp.repeat(live_here, page) == 1) & jnp.any(positions[:, None] == starts[None, :], axis=1)
    count = jnp.cumsum(resets.astype(jnp.int32))
    cnt_col = count.reshape(rows, 1)
    cnt_row = count.reshape(-1, 1, page)
    last = count.reshape(-1, page)[:, -1]
    if line:
        *mixer_rows, normed, cnt_col, cnt_row, last = lax.optimization_barrier(
            (*mixer_rows, normed, cnt_col, cnt_row, last)
        )
    w_in, w_out = Rows(mixer_rows, 0, 3 * cols), Rows(mixer_rows, 3 * cols)

    half_rows = pages * page // 2
    table_half = lax.dynamic_slice_in_dim(page_table, rep_index * (pages // 2), pages // 2, 0)
    token_cols = lax.dynamic_slice_in_dim(token_pages, mp_index * kwide, kwide, 2)
    ordered = jnp.take(token_cols, table_half, axis=0).reshape(half_rows, kwide)

    qs, ks, v, fin, pack = project(
        ids, live_here, last, normed, foreign, w_in, decay_floor.reshape(1, cols), cnt_col
    )
    earlier = [lax.ppermute(pack, "ctx", [(1, 2)])] if line else from_earlier(pack, ctx_count)
    terms = mix(ids, last, earlier, qs, ks, v, fin, w_out, cnt_col, cnt_row)
    if line:
        theirs, stage = sum_scatter(terms[2:])
        back = lax.ppermute(theirs.astype(BF), "ctx", [(1, 0), (2, 3)])
        keep, send, *_ = lax.optimization_barrier((terms[0], terms[1], *stage))
        mixed = jnp.where(middle, sum_scatter((keep, send))[0], back.astype(F32))
    else:
        mixed = sum_scatter(terms)[0]
    residual = ordered.astype(F32) + mixed
    mine, other = gather_plane(residual.astype(BF))
    down_terms = feed_forward(ids, mine, other, feed_gain.reshape(4, 1, kwide), w_feed, feed)
    summed = residual + sum_scatter(down_terms)[0]
    live_half = jnp.repeat(
        lax.dynamic_slice_in_dim(live_flags, rep_index * (pages // 2), pages // 2, 0), page
    )
    return jnp.where(live_half[:, None] == 1, summed, 0.0).astype(BF)


def solution(mesh):
    in_specs = (
        P("ctx", None, None),
        P("ctx"),
        P("ctx"),
        P(),
        P(("mp", "rep")),
        P(),
        P(),
        P(None, ("ctx", "mp"), None),
        P(None, ("ctx", "mp")),
        P(None, ("ctx", "mp"), None),
        P(None, ("ctx", "mp")),
    )
    out_specs = P(("ctx", "rep"), "mp")
    return jax.shard_map(shards, mesh=mesh, in_specs=in_specs, out_specs=out_specs, check_vma=False)
```

```python
import functools

import jax
import jax.numpy as jnp
from jax import lax
from jax.experimental import pallas as pl
from jax.experimental.pallas import tpu as pltpu
from jax.sharding import PartitionSpec as P

HEAD = 128
EPS = 1e-05
BF = jnp.bfloat16
F32 = jnp.float32
VMEM_LIMIT = 48 * 1024 * 1024


def nt(a, b):
    return lax.dot_general(a, b, (((1,), (1,)), ((), ())), preferred_element_type=F32)


def tn(a, b):
    return lax.dot_general(a, b, (((0,), (0,)), ((), ())), preferred_element_type=F32)


def nn(a, b):
    return jnp.dot(a, b, preferred_element_type=F32)


def sigmoid(v):
    return 1.0 / (1.0 + jnp.exp(-v))


def call(body, grid, in_specs, out_specs, out_shape, scratch=(), prefetch=1, cost=None):
    return pl.pallas_call(
        body,
        out_shape=out_shape,
        grid_spec=pltpu.PrefetchScalarGridSpec(
            num_scalar_prefetch=prefetch,
            grid=grid,
            in_specs=in_specs,
            out_specs=out_specs,
            scratch_shapes=list(scratch),
        ),
        compiler_params=pltpu.CompilerParams(
            dimension_semantics=("arbitrary",) * len(grid), vmem_limit_bytes=VMEM_LIMIT
        ),
        cost_estimate=None
        if cost is None
        else pl.CostEstimate(flops=cost[0], bytes_accessed=cost[1], transcendentals=0),
    )


def whole(shape):
    zeros = (0,) * len(shape)
    return pl.BlockSpec(shape, lambda *_: zeros, pipeline_mode=pl.Buffered(1))


ANY = pl.BlockSpec(memory_space=pl.ANY)


class Rows:
    def __init__(self, arrays, low=0, high=None):
        self.arrays = list(arrays)
        self.planes, self.rows, columns = (
            self.arrays[0].shape if len(self.arrays) == 1 else (4, *self.arrays[0].shape)
        )
        self.part = slice(low, columns if high is None else high)
        self.scratch = [
            pltpu.VMEM((self.planes * self.rows, self.part.stop - low), BF),
            pltpu.SemaphoreType.DMA((self.planes * 4,)),
        ]

    def copies(self, ids_ref, refs, held, sems, plane, ref):
        rows = self.rows // 4
        to_plane = plane if len(refs) == 1 else ids_ref[(9 if len(refs) == 6 else 3) + plane]
        for s in range(4):
            to = pl.multiple_of((to_plane * 4 + (ids_ref[0] ^ s)) * rows, rows)
            yield pltpu.make_async_copy(
                ref.at[pl.ds(s * rows, rows), self.part], held.at[pl.ds(to, rows)], sems.at[4 * plane + s]
            )

    def start(self, ids_ref, refs, held, sems):
        def begin(plane, ref):
            for copy in self.copies(ids_ref, refs, held, sems, plane, ref):
                copy.start()

        for plane in range(self.planes):
            if len(refs) == 6 and plane >= 2:
                pl.when(ids_ref[2] == 1)(functools.partial(begin, plane, refs[2 * plane - 2]))
                pl.when(ids_ref[2] == 0)(functools.partial(begin, plane, refs[2 * plane - 1]))
            else:
                begin(plane, refs[0].at[plane] if len(refs) == 1 else refs[plane])

    def wait(self, ids_ref, refs, held, sems):
        for plane in range(self.planes):
            ref = refs[0].at[plane] if len(refs) == 1 else refs[plane]
            for copy in self.copies(ids_ref, refs, held, sems, plane, ref):
                copy.wait()


def pack_mixer(ids, mixer_in, mixer_out):
    width = mixer_in.shape[1]
    cols = mixer_in.shape[2] // 8

    def body(ids_ref, q_ref, f_ref, v_ref, o_ref, out_ref):
        out_ref[0, :, 0:cols] = q_ref[0].astype(BF)
        out_ref[0, :, cols : 2 * cols] = f_ref[0].astype(BF)
        out_ref[0, :, 2 * cols : 3 * cols] = v_ref[0].astype(BF)
        out_ref[0, :, 3 * cols : 4 * cols] = o_ref[...].T.astype(BF)

    def dest(s, ids_ref):
        return 2 * (ids_ref[0] ^ s) + ids_ref[1]

    def part(i):
        return pl.BlockSpec((1, width, cols), lambda s, r: (i, 0, dest(s, r)))

    return call(
        body,
        (4,),
        [part(0), part(1), part(2), pl.BlockSpec((cols, width), lambda s, r: (dest(s, r), 0))],
        pl.BlockSpec((1, width, 4 * cols), lambda s, r: (s, 0, 0)),
        jax.ShapeDtypeStruct((4, width, 4 * cols), BF),
        cost=(0, 4 * width * cols * 24),
    )(ids, mixer_in, mixer_in, mixer_in, mixer_out)


class Feed:
    def __init__(self, hidden_all):
        tiles = hidden_all // 128 // 8
        self.half_at = 8 * tiles
        assert hidden_all == (8 * tiles + 4) * 128
        self.near = tiles * 128
        self.near_up = 2 * self.near + 128
        self.units = self.near + 128


def pack_feed(ids, gate_up, down, feed):
    width = gate_up.shape[1]
    near, up = feed.near, feed.near_up
    shapes = [(width, up), (near + 64, width)]

    def body(ids_ref, *refs):
        g_ref, u_ref, gh_ref, uh_ref, d_ref, dh_ref, out_ref, down_ref = refs
        odd = (ids_ref[0] ^ pl.program_id(0)) % 2
        out_ref[0, :, 0:near] = g_ref[0].astype(BF)
        lane = lax.broadcasted_iota(jnp.int32, (width, 128), 1)
        gh, uh = gh_ref[0], uh_ref[0]
        even_mix = jnp.where(lane < 64, gh, pltpu.roll(uh, 64, 1))
        odd_mix = jnp.where(lane < 64, pltpu.roll(gh, 64, 1), uh)
        out_ref[0, :, near : near + 128] = jnp.where(odd == 1, odd_mix, even_mix).astype(BF)
        out_ref[0, :, near + 128 : up] = u_ref[0].astype(BF)
        down_ref[0, 0:near] = d_ref[...].astype(BF)
        down_ref[0, near : near + 64] = dh_ref[...].astype(BF)

    def dest(s, r):
        return 4 * r[1] + (r[0] ^ s)

    def tile(s, r):
        return feed.half_at + 2 * r[1] + (r[0] ^ s) // 2

    def cols(i):
        return pl.BlockSpec((1, width, near), lambda s, r: (i, 0, dest(s, r)))

    def mix(i):
        return pl.BlockSpec((1, width, 128), lambda s, r: (i, 0, tile(s, r)))

    in_specs = [
        cols(0),
        cols(1),
        mix(0),
        mix(1),
        pl.BlockSpec((near, width), lambda s, r: (dest(s, r), 0)),
        pl.BlockSpec((64, width), lambda s, r: (2 * feed.half_at + dest(s, r), 0)),
    ]
    args = [gate_up, gate_up, gate_up, gate_up, down, down]
    return call(
        body,
        (4,),
        in_specs,
        [pl.BlockSpec((1, *shape), lambda s, r: (s, 0, 0)) for shape in shapes],
        [jax.ShapeDtypeStruct((4, *shape), BF) for shape in shapes],
        cost=(0, 4 * width * (up + near + 64) * 6),
    )(ids, *args)


def mp_perm(value, s):
    return lax.ppermute(value, "mp", [(i, i ^ s) for i in range(4)])


def rep_perm(value):
    return lax.ppermute(value, "rep", [(0, 1), (1, 0)])


def across_plane(packed):
    moved = [mp_perm(packed[s], s) for s in (1, 2, 3)]
    return jnp.concatenate([packed[0], *moved], axis=0), moved


def after(value, *others):
    return lax.optimization_barrier((value, *others))[0]


def from_earlier(value, count):
    return [
        lax.ppermute(value, "ctx", [(i, i + d) for i in range(count - d)]) for d in range(1, count)
    ]


def total_before(value, count):
    shift = 1
    total = lax.ppermute(value, "ctx", [(i, i + 1) for i in range(count - 1)])
    so_far = total + value
    while 2 * shift < count:
        came = lax.ppermute(so_far, "ctx", [(i, i + 2 * shift) for i in range(count - 2 * shift)])
        total, so_far, shift = total + came, so_far + came, 2 * shift
    return total


def normalise(table, token_pages, gain):
    _, page, width = token_pages.shape
    pages = table.shape[0]

    def body(table_ref, x_ref, g_ref, out_ref):
        x = x_ref[0].astype(F32)
        scale = lax.rsqrt(jnp.mean(x * x, axis=-1, keepdims=True) + EPS)
        out_ref[...] = (x * scale * g_ref[...]).astype(BF)

    return call(
        body,
        (pages,),
        [pl.BlockSpec((1, page, width), lambda i, t: (t[i], 0, 0)), whole((1, width))],
        pl.BlockSpec((page, width), lambda i, t: (i, 0)),
        jax.ShapeDtypeStruct((pages * page, width), BF),
        cost=(pages * page * width * 4, pages * page * width * 4),
    )(table, token_pages, gain.reshape(1, width))


def step_state(state, ks, v, same_last, keep, final):
    update = tn(v, jnp.where(same_last, ks, jnp.zeros_like(ks)))
    return (jnp.where(keep, state, 0.0) + update) * final


def project(ids, live, last, normed, foreign, weights, floor, cnt_col):
    width = normed.shape[1]
    cols = floor.shape[1]
    heads = cols // HEAD
    pages = live.shape[0]
    rows = cnt_col.shape[0]
    page = rows // pages
    group = 4
    steps = pages // group

    n = len(weights.arrays)

    def body(ids_ref, *refs):
        pl.when(ids_ref[2] == 1)(lambda: work(ids_ref, *refs))

    def work(ids_ref, live_ref, last_ref, x_ref, *refs):
        f_refs, refs = refs[: len(foreign)], refs[len(foreign) :]
        w_refs = refs[:n]
        fl_ref, cnt_ref, qs_ref, ks_ref, v_ref, fin_ref, st_ref, state, total, held, sems = refs[n:]
        step = pl.program_id(0)

        @pl.when(step == 0)
        def _():
            weights.start(ids_ref, w_refs, held, sems)
            state[...] = jnp.zeros_like(state)
            total[...] = jnp.zeros_like(total)
            weights.wait(ids_ref, w_refs, held, sems)

        x = x_ref[...]
        if foreign:
            core, y = ids_ref[0] & 1, ids_ref[0] >> 1
            tiles = []
            for q in range(group):
                near, far = ([f[:, 0, dy].reshape(page, width) for dy in range(2)] for f in f_refs)
                row = [jnp.where(core == q % 2, a, b) for a, b in zip(near, far)]
                tiles.append(jnp.where(y == q // 2, row[0], row[1]))
            x = jnp.where((step >> 1) == ids_ref[8], x, jnp.concatenate(tiles, axis=0))
        proj = nn(x, held[...])
        row = lax.broadcasted_iota(jnp.int32, (page, page), 0)
        col = lax.broadcasted_iota(jnp.int32, (page, page), 1)
        lower = (row >= col).astype(F32)
        floor_row = fl_ref[...]
        for j in range(group):
            p = step * group + j
            here = slice(j * page, (j + 1) * page)
            alive = live_ref[p].astype(F32)
            now = last_ref[p]
            before = jnp.where(p == 0, 0, last_ref[jnp.maximum(p - 1, 0)])
            q = proj[here, 0:cols]
            q = q * sigmoid(q)
            f = proj[here, cols : 2 * cols]
            gate = sigmoid(f)
            forget = floor_row + (1.0 - floor_row) * gate
            key = (1.0 - forget) * alive
            log_decay = jnp.log(forget) * alive
            cum = jnp.dot(lower, log_decay, precision=lax.Precision.HIGHEST, preferred_element_type=F32)
            final_log = cum[page - 1 : page, :]
            final = jnp.exp(final_log)
            ks = (key * jnp.exp(-cum)).astype(BF)
            v = proj[here, 2 * cols : 3 * cols].astype(BF)
            qs_ref[here, :] = (q * jnp.exp(cum)).astype(BF)
            ks_ref[here, :] = ks
            v_ref[here, :] = v
            fin_ref[j] = final
            total[...] += final_log
            same_last = cnt_ref[here, :] == now
            for h in range(heads):
                hc = slice(h * HEAD, (h + 1) * HEAD)
                state[h] = step_state(state[h], ks[:, hc], v[:, hc], same_last, now == before, final[:, hc])

        @pl.when(step == steps - 1)
        def _():
            none = last_ref[pages - 1] == 0
            decay = jnp.where(none, jnp.exp(total[...]), 0.0)
            for h in range(heads):
                st_ref[h, 0:HEAD, :] = state[h].astype(BF)
                st_ref[h, HEAD : HEAD + 16, :] = jnp.broadcast_to(
                    decay[:, h * HEAD : (h + 1) * HEAD], (16, HEAD)
                ).astype(BF)

    block = group * page
    return call(
        body,
        (steps,),
        [
            pl.BlockSpec((block, width), lambda i, *_: (i & 1, 0)),
        ]
        + [
            pl.BlockSpec(
                (2, 1, 2, page // 2, width), lambda i, r, *_: (0, (i & 1) ^ r[1], 0, 0, 0)
            )
        ]
        * len(foreign)
        + [ANY] * n
        + [
            whole((1, cols)),
            pl.BlockSpec((block, 1), lambda i, *_: (i, 0)),
        ],
        [
            pl.BlockSpec((block, cols), lambda i, *_: (i, 0)),
            pl.BlockSpec((block, cols), lambda i, *_: (i, 0)),
            pl.BlockSpec((block, cols), lambda i, *_: (i, 0)),
            pl.BlockSpec((group, 1, cols), lambda i, *_: (i, 0, 0)),
            whole((heads, HEAD + 16, HEAD)),
        ],
        [
            jax.ShapeDtypeStruct((rows, cols), BF),
            jax.ShapeDtypeStruct((rows, cols), BF),
            jax.ShapeDtypeStruct((rows, cols), BF),
            jax.ShapeDtypeStruct((pages, 1, cols), F32),
            jax.ShapeDtypeStruct((heads, HEAD + 16, HEAD), BF),
        ],
        scratch=[pltpu.VMEM((heads, HEAD, HEAD), F32), pltpu.VMEM((1, cols), F32), *weights.scratch],
        prefetch=3,
        cost=(2 * rows * width * 3 * cols, rows * width * 2 + width * cols * 8),
    )(ids, live, last, normed, *foreign, *weights.arrays, floor, cnt_col)


def mix(ids, last, earlier, qs, ks, v, fin, weights, cnt_col, cnt_row):
    rows, cols = qs.shape
    heads = cols // HEAD
    pages = fin.shape[0]
    page = rows // pages
    group = 4
    steps = pages // group
    width = weights.planes * weights.rows
    n = len(earlier)
    spans = steps // 2
    m = n + 4 + len(weights.arrays)

    def body(ids_ref, *refs):
        pl.when(ids_ref[2] == 1)(lambda: work(ids_ref, *refs))

    def work(ids_ref, last_ref, *refs):
        packs = refs[:n]
        qs_ref, ks_ref, v_ref, fin_ref = refs[n : n + 4]
        w_refs = refs[n + 4 : m]
        cc_ref, cr_ref = refs[m : m + 2]
        outs = refs[m + 2 : m + 2 + 2 * spans]
        state, held, sems = refs[m + 2 + 2 * spans :]
        step = pl.program_id(0)

        @pl.when(step == 0)
        def _():
            weights.start(ids_ref, w_refs, held, sems)
            for h in range(heads):
                total = jnp.zeros((HEAD, HEAD), F32)
                for pack in reversed(packs):
                    total = total * pack[h, HEAD : HEAD + 1, :].astype(F32) + pack[h, 0:HEAD, :].astype(F32)
                state[h] = total

        row = lax.broadcasted_iota(jnp.int32, (page, page), 0)
        col = lax.broadcasted_iota(jnp.int32, (page, page), 1)
        lower = row >= col
        normed = []
        for j in range(group):
            p = step * group + j
            here = slice(j * page, (j + 1) * page)
            now = last_ref[p]
            before = jnp.where(p == 0, 0, last_ref[jnp.maximum(p - 1, 0)])
            cc, cr = cc_ref[here, :], cr_ref[j]
            allowed = lower & (cc == cr)
            reached = cc == before
            same_last = cc == now
            for h in range(heads):
                hc = slice(h * HEAD, (h + 1) * HEAD)
                q_h, k_h, v_h = qs_ref[here, hc], ks_ref[here, hc], v_ref[here, hc]
                scores = jnp.where(allowed, nt(q_h, k_h), 0.0).astype(BF)
                out = nn(scores, v_h)
                out = out + jnp.where(reached, nt(q_h, state[h].astype(BF)), 0.0)
                state[h] = step_state(state[h], k_h, v_h, same_last, now == before, fin_ref[j, :, hc])
                scale = lax.rsqrt(jnp.mean(out * out, axis=-1, keepdims=True) + EPS)
                normed.append((out * scale).astype(BF))
        hn = jnp.concatenate(
            [jnp.concatenate(normed[j * heads : (j + 1) * heads], axis=1) for j in range(group)], axis=0
        )

        @pl.when(step == 0)
        def _():
            weights.wait(ids_ref, w_refs, held, sems)

        for dc in range(2):
            for dy in range(2):
                term = nt(hn, held[block_of(ids_ref[0] ^ (2 * dy + dc), width // 4), :]).astype(BF)
                for span in range(spans):

                    @pl.when((step // 2) ^ ids_ref[8] == span)
                    def _(span=span, dc=dc, dy=dy, term=term):
                        outs[2 * span + dc][:, 0, dy] = term.reshape(2, block // 2, width // 4)

    block = group * page
    rowspec = pl.BlockSpec((block, cols), lambda i, *_: (i, 0))

    def terms(span):
        def index(i, r, l):
            low = 2 * (span ^ r[8])
            i = jnp.minimum(jnp.maximum(i, low), low + 1) & 1
            return (0, i ^ r[1], 0, 0, 0)

        return pl.BlockSpec((2, 1, 2, block // 2, width // 4), index)

    return call(
        body,
        (steps,),
        [whole(e.shape) for e in earlier]
        + [
            rowspec,
            rowspec,
            rowspec,
            pl.BlockSpec((group, 1, cols), lambda i, *_: (i, 0, 0)),
        ]
        + [ANY] * len(weights.arrays)
        + [
            pl.BlockSpec((block, 1), lambda i, *_: (i, 0)),
            pl.BlockSpec((group, 1, page), lambda i, *_: (i, 0, 0)),
        ],
        [terms(span) for span in range(spans) for _ in range(2)],
        [jax.ShapeDtypeStruct((2, 2, 2, block // 2, width // 4), BF)] * (2 * spans),
        scratch=[pltpu.VMEM((heads, HEAD, HEAD), F32), *weights.scratch],
        prefetch=2,
        cost=(2 * rows * cols * width, rows * width * 2),
    )(ids, last, *earlier, qs, ks, v, fin, *weights.arrays, cnt_col, cnt_row)


def add(a, b):
    return (a.astype(F32) + b.astype(F32)).astype(BF)


def sum_scatter(terms, *others):
    mine, other = terms[0], mp_perm(terms[1], 1)
    a_keep, a_send = add(mine[0, 0], other[0, 0]), add(mine[0, 1], other[0, 1])
    b_keep, b_send = add(mine[1, :, 0], other[1, :, 0]), add(mine[1, :, 1], other[1, :, 1])
    a_came, b_came = rep_perm(a_send), mp_perm(b_send, 2)
    a_came = after(a_came, *others)
    a_send, b_send = add(a_keep[1], a_came[1]), add(b_keep[1], b_came[1])
    a_last, b_last = mp_perm(a_send, 2), rep_perm(b_send)
    a = a_keep[0].astype(F32) + a_came[0].astype(F32) + a_last.astype(F32)
    b = b_keep[0].astype(F32) + b_came[0].astype(F32) + b_last.astype(F32)
    return jnp.concatenate([a, b], axis=0), (a_came, b_came)


def gather_plane(value, *others):
    half = value.shape[0] // 2
    a, b = value[:half], value[half:]
    a_y, b_x = mp_perm(a, 2), rep_perm(b)
    a_pair, b_pair = jnp.stack([a, a_y]), jnp.stack([b, b_x])
    a_x, b_y = rep_perm(a_pair), mp_perm(b_pair, 2)
    mine = jnp.stack([jnp.stack([a_pair, a_x]), jnp.stack([b_pair, b_y], axis=1)])
    mine = after(mine, *others)
    return mine, mp_perm(mine, 1)


def block_of(k, rows):
    return pl.ds(pl.multiple_of(k * rows, rows), rows)


def feed_up(ids, mine, other, gain, weights, feed):
    near, up, units = feed.near, feed.near_up, feed.units
    rows, kwide = mine.shape[-2:]
    width = 4 * kwide
    n = len(weights.arrays)
    places = [(dy, dc) for dy in range(2) for dc in range(2)]

    def body(ids_ref, m_ref, o_ref, g_ref, *rest):
        w_refs, (out_ref, x_ref, held, sems) = rest[:n], rest[n:]
        first = pl.program_id(0) == 0
        pl.when(first)(lambda: weights.start(ids_ref, w_refs, held, sems))
        blocks = [(m_ref, o_ref)[dc][0, 0, dy].astype(F32) for dy, dc in places]
        square = sum(jnp.sum(b * b, axis=-1, keepdims=True) for b in blocks)
        scale = lax.rsqrt(square / width + EPS)
        for (dy, dc), b in zip(places, blocks):
            k = ids_ref[0] ^ (2 * dy + dc)
            x_ref[:, block_of(k, kwide)] = (b * scale * g_ref[k]).astype(BF)
        pl.when(first)(lambda: weights.wait(ids_ref, w_refs, held, sems))

        x = x_ref[...]
        h = nn(x, held[...])
        gate, edge, upward = h[:, 0:near], h[:, near : near + 128], h[:, near + 128 : up]
        out_ref[0, 0, :, 0:near] = (gate * sigmoid(gate) * upward).astype(BF)
        mixed = edge * sigmoid(edge) * pltpu.roll(edge, 64, 1)
        lane = lax.broadcasted_iota(jnp.int32, mixed.shape, 1)
        out_ref[0, 0, :, near:units] = jnp.where(lane < 64, mixed, 0.0).astype(BF)

    spec = pl.BlockSpec((1, 1, 2, rows, kwide), lambda i, r: (i % 2, i // 2, 0, 0, 0))
    return call(
        body,
        (4,),
        [spec, spec, whole(gain.shape)] + [ANY] * n,
        pl.BlockSpec((1, 1, rows, units), lambda i, r: (i % 2, i // 2, 0, 0)),
        jax.ShapeDtypeStruct((2, 2, rows, units), BF),
        scratch=[pltpu.VMEM((rows, width), BF), *weights.scratch],
        cost=(8 * rows * width * up, width * up * 2 + 16 * rows * width),
    )(ids, mine, other, gain, *weights.arrays)


def feed_down(ids, hidden, weights, kwide, dc):
    rows, units = hidden.shape[-2:]
    used = units - 64
    parts = 4 if weights.ndim == 3 else 1

    def body(ids_ref, h_ref, w_ref, out_ref, held, sems):
        def copies():
            for dy in range(2):
                k = ids_ref[0] ^ (2 * dy + dc)
                for s in range(parts):
                    if parts == 1:
                        ref, to = w_ref.at[:, block_of(k, kwide)], dy * kwide
                    else:
                        ref = w_ref.at[k, pl.ds(s * used, used)]
                        to = pl.multiple_of(dy * kwide + (ids_ref[0] ^ s) * (kwide // 4), 128)
                    to = held.at[pl.ds(0, used), pl.ds(to, kwide // parts)]
                    yield pltpu.make_async_copy(ref, to, sems.at[parts * dy + s])

        @pl.when(pl.program_id(0) == 0)
        def _():
            for copy in copies():
                copy.start()
            held[used:units, :] = jnp.zeros((units - used, 2 * kwide), BF)
            for copy in copies():
                copy.wait()

        term = nn(h_ref[0, 0], held[...]).astype(BF)
        for dy in range(2):
            out_ref[0, 0, dy] = term[:, dy * kwide : (dy + 1) * kwide]

    return call(
        body,
        (4,),
        [pl.BlockSpec((1, 1, rows, units), lambda i, r: (i % 2, i // 2, 0, 0)), ANY],
        pl.BlockSpec((1, 1, 2, rows, kwide), lambda i, r: (i % 2, i // 2, 0, 0, 0)),
        jax.ShapeDtypeStruct((2, 2, 2, rows, kwide), BF),
        scratch=[pltpu.VMEM((units, 2 * kwide), BF), pltpu.SemaphoreType.DMA((2 * parts,))],
        cost=(16 * rows * kwide * units, 4 * kwide * units + 16 * rows * kwide),
    )(ids, hidden, weights)


def shards(
    token_pages,
    page_table,
    live_flags,
    lengths,
    decay_floor,
    mixer_gain,
    feed_gain,
    trainer_mixer_in,
    trainer_mixer_out,
    trainer_gate_up,
    trainer_down,
):
    ctx_count = lax.axis_size("ctx")
    ctx_index = lax.axis_index("ctx")
    mp_index = lax.axis_index("mp")
    rep_index = lax.axis_index("rep")
    pages, page, width = token_pages.shape
    cols = decay_floor.shape[0]
    kwide = width // 4
    feed = Feed(trainer_gate_up.shape[2])
    line = ctx_count == 4 and pages == 8
    middle = (ctx_index == 1) | (ctx_index == 2)
    beyond = jnp.where(ctx_index == 1, 0, 3)
    order = [ctx_index, 3 - ctx_index, beyond, 3 - beyond]
    own_span = (ctx_index == 1).astype(jnp.int32) if line else 0
    active = middle.astype(jnp.int32) if line else 1
    sources = [ctx_index, ctx_index ^ 1, ctx_index ^ jnp.where(middle, 3, 2), ctx_index ^ jnp.where(middle, 2, 3)]
    ids = jnp.stack([mp_index, rep_index, active, *order, ctx_index, own_span, *sources]).astype(jnp.int32)

    def gather(value):
        return Rows([lax.all_gather(value, "ctx", axis=0)])

    packed_mixer = pack_mixer(ids, trainer_mixer_in, trainer_mixer_out)
    plane_mixer, moved = across_plane(packed_mixer)
    packed_up, packed_down = pack_feed(after(ids, plane_mixer), trainer_gate_up, trainer_down, feed)
    plane_up, moved_up = across_plane(after(packed_up, *moved))
    plane_down, _ = across_plane(after(packed_down, *moved_up))
    flags = after(live_flags, packed_mixer)
    if line:
        sent = lax.dynamic_slice_in_dim(page_table, rep_index * 4 + mp_index, 1, 0)
        chunk = normalise(after(sent, packed_mixer), token_pages, mixer_gain)
        chunk = lax.ppermute(chunk, "ctx", [(0, 1), (3, 2)])
        spread = jnp.broadcast_to(flags[:, None], (pages, 128)).astype(jnp.int32)
        came = lax.ppermute(spread, "ctx", [(0, 1), (3, 2)])
        totals = jnp.broadcast_to(jnp.sum(spread + came, axis=0, keepdims=True), (8, 128))
        totals = lax.ppermute(totals, "ctx", [(1, 2)])
        base = after(totals, plane_mixer)[0, 0]
        theirs = came[:, 0]
        live_here = jnp.concatenate(
            [jnp.where(ctx_index == 1, theirs, flags), jnp.where(ctx_index == 1, flags, theirs)]
        )
        page_start = (base + jnp.cumsum(live_here) - live_here) * page

        plane_mixer = after(plane_mixer, came, totals)
        across = lax.ppermute(plane_mixer, "ctx", [(1, 2), (2, 1)])
        inward = lax.ppermute(plane_mixer, "ctx", [(0, 1), (3, 2)])
        across, inward = lax.optimization_barrier((across, inward))
        onward = lax.ppermute(inward, "ctx", [(1, 2), (2, 1)])
        mixer_rows = [plane_mixer, across, inward, onward]
        plane_up = after(plane_up, onward)
        normed = normalise(after(page_table, plane_mixer), token_pages, mixer_gain)
        foreign = gather_plane(after(chunk, plane_mixer), across, inward, normed)
    else:
        normed = normalise(page_table, token_pages, mixer_gain)
        foreign = ()
        live_here = flags
        live_total = jnp.broadcast_to(jnp.sum(flags) * page, (8, 128)).astype(jnp.int32)
        page_start = total_before(live_total, ctx_count)[0, 0] + (jnp.cumsum(flags) - flags) * page
        mixer_rows = gather(plane_mixer).arrays
    w_up = gather(plane_up)
    w_down = lax.all_gather(plane_down, "ctx", axis=0)
    if kwide // 4 % 128 or ctx_count != 4:
        parts = w_down.reshape(ctx_count, 4, -1, w_down.shape[-1])
        parts = jnp.take(parts, mp_index ^ jnp.arange(4), axis=1)
        w_down = jnp.transpose(parts, (2, 0, 1, 3)).reshape(-1, width)

    rows = live_here.shape[0] * page
    positions = (page_start[:, None] + jnp.arange(page, dtype=jnp.int32)[None, :]).reshape(rows)
    lengths = after(lengths, plane_mixer)
    starts = jnp.cumsum(lengths) - lengths
    resets = (jnp.repeat(live_here, page) == 1) & jnp.any(positions[:, None] == starts[None, :], axis=1)
    count = jnp.cumsum(resets.astype(jnp.int32))
    cnt_col = count.reshape(rows, 1)
    cnt_row = count.reshape(-1, 1, page)
    last = count.reshape(-1, page)[:, -1]
    if line:
        *mixer_rows, normed, cnt_col, cnt_row, last = lax.optimization_barrier(
            (*mixer_rows, normed, cnt_col, cnt_row, last)
        )
    w_in, w_out = Rows(mixer_rows, 0, 3 * cols), Rows(mixer_rows, 3 * cols)

    half_rows = pages * page // 2
    table_half = lax.dynamic_slice_in_dim(page_table, rep_index * (pages // 2), pages // 2, 0)
    token_cols = lax.dynamic_slice_in_dim(token_pages, mp_index * kwide, kwide, 2)
    ordered = jnp.take(token_cols, table_half, axis=0).reshape(half_rows, kwide)

    qs, ks, v, fin, pack = project(
        ids, live_here, last, normed, foreign, w_in, decay_floor.reshape(1, cols), cnt_col
    )
    if line:
        earlier = [lax.ppermute(pack, "ctx", [(1, 2)])]
    else:
        earlier = from_earlier(pack, ctx_count)
    terms = mix(ids, last, earlier, qs, ks, v, fin, w_out, cnt_col, cnt_row)
    if line:
        theirs, stage = sum_scatter(terms[2:])
        back = lax.ppermute(theirs.astype(BF), "ctx", [(1, 0), (2, 3)])
        keep, send, *_ = lax.optimization_barrier((terms[0], terms[1], *stage))
        mixed = jnp.where(middle, sum_scatter((keep, send))[0], back.astype(F32))
    else:
        mixed = sum_scatter(terms)[0]
    residual = ordered.astype(F32) + mixed
    mine, other = gather_plane(residual.astype(BF))
    hidden = feed_up(ids, mine, other, feed_gain.reshape(4, 1, kwide), w_up, feed)
    send = feed_down(ids, hidden, w_down, kwide, 1)
    summed = residual + sum_scatter((feed_down(ids, hidden, w_down, kwide, 0), send))[0]
    live_half = jnp.repeat(
        lax.dynamic_slice_in_dim(live_flags, rep_index * (pages // 2), pages // 2, 0), page
    )
    return jnp.where(live_half[:, None] == 1, summed, 0.0).astype(BF)


def solution(mesh):
    in_specs = (
        P("ctx", None, None),
        P("ctx"),
        P("ctx"),
        P(),
        P(("mp", "rep")),
        P(),
        P(),
        P(None, ("ctx", "mp"), None),
        P(None, ("ctx", "mp")),
        P(None, ("ctx", "mp"), None),
        P(None, ("ctx", "mp")),
    )
    out_specs = P(("ctx", "rep"), "mp")
    return jax.shard_map(shards, mesh=mesh, in_specs=in_specs, out_specs=out_specs, check_vma=False)
```

```python
import functools

import jax
import jax.numpy as jnp
from jax import lax
from jax.experimental import pallas as pl
from jax.experimental.pallas import tpu as pltpu
from jax.sharding import PartitionSpec as P

HEAD = 128
EPS = 1e-05
BF = jnp.bfloat16
F32 = jnp.float32
VMEM_LIMIT = 48 * 1024 * 1024
FEED_LIMIT = 62 * 1024 * 1024


def nt(a, b):
    return lax.dot_general(a, b, (((1,), (1,)), ((), ())), preferred_element_type=F32)


def tn(a, b):
    return lax.dot_general(a, b, (((0,), (0,)), ((), ())), preferred_element_type=F32)


def nn(a, b):
    return jnp.dot(a, b, preferred_element_type=F32)


def sigmoid(v):
    return 1.0 / (1.0 + jnp.exp(-v))


def call(body, grid, in_specs, out_specs, out_shape, scratch=(), prefetch=1, cost=None, limit=VMEM_LIMIT):
    return pl.pallas_call(
        body,
        out_shape=out_shape,
        grid_spec=pltpu.PrefetchScalarGridSpec(
            num_scalar_prefetch=prefetch,
            grid=grid,
            in_specs=in_specs,
            out_specs=out_specs,
            scratch_shapes=list(scratch),
        ),
        compiler_params=pltpu.CompilerParams(
            dimension_semantics=("arbitrary",) * len(grid), vmem_limit_bytes=limit
        ),
        cost_estimate=None
        if cost is None
        else pl.CostEstimate(flops=cost[0], bytes_accessed=cost[1], transcendentals=0),
    )


def whole(shape):
    zeros = (0,) * len(shape)
    return pl.BlockSpec(shape, lambda *_: zeros, pipeline_mode=pl.Buffered(1))


ANY = pl.BlockSpec(memory_space=pl.ANY)


class Rows:
    def __init__(self, arrays, low=0, high=None):
        self.arrays = list(arrays)
        self.planes, self.rows, columns = (
            self.arrays[0].shape if len(self.arrays) == 1 else (4, *self.arrays[0].shape)
        )
        self.part = slice(low, columns if high is None else high)
        self.scratch = [
            pltpu.VMEM((self.planes * self.rows, self.part.stop - low), BF),
            pltpu.SemaphoreType.DMA((self.planes * 4,)),
        ]

    def copies(self, ids_ref, refs, held, sems, plane, ref):
        rows = self.rows // 4
        to_plane = plane if len(refs) == 1 else ids_ref[(9 if len(refs) == 6 else 3) + plane]
        for s in range(4):
            to = pl.multiple_of((to_plane * 4 + (ids_ref[0] ^ s)) * rows, rows)
            yield pltpu.make_async_copy(
                ref.at[pl.ds(s * rows, rows), self.part], held.at[pl.ds(to, rows)], sems.at[4 * plane + s]
            )

    def start(self, ids_ref, refs, held, sems):
        def begin(plane, ref):
            for copy in self.copies(ids_ref, refs, held, sems, plane, ref):
                copy.start()

        for plane in range(self.planes):
            if len(refs) == 6 and plane >= 2:
                pl.when(ids_ref[2] == 1)(functools.partial(begin, plane, refs[2 * plane - 2]))
                pl.when(ids_ref[2] == 0)(functools.partial(begin, plane, refs[2 * plane - 1]))
            else:
                begin(plane, refs[0].at[plane] if len(refs) == 1 else refs[plane])

    def wait(self, ids_ref, refs, held, sems):
        for plane in range(self.planes):
            ref = refs[0].at[plane] if len(refs) == 1 else refs[plane]
            for copy in self.copies(ids_ref, refs, held, sems, plane, ref):
                copy.wait()


def pack_mixer(ids, mixer_in, mixer_out):
    width = mixer_in.shape[1]
    cols = mixer_in.shape[2] // 8

    def body(ids_ref, q_ref, f_ref, v_ref, o_ref, out_ref):
        out_ref[0, :, 0:cols] = q_ref[0].astype(BF)
        out_ref[0, :, cols : 2 * cols] = f_ref[0].astype(BF)
        out_ref[0, :, 2 * cols : 3 * cols] = v_ref[0].astype(BF)
        out_ref[0, :, 3 * cols : 4 * cols] = o_ref[...].T.astype(BF)

    def dest(s, ids_ref):
        return 2 * (ids_ref[0] ^ s) + ids_ref[1]

    def part(i):
        return pl.BlockSpec((1, width, cols), lambda s, r: (i, 0, dest(s, r)))

    return call(
        body,
        (4,),
        [part(0), part(1), part(2), pl.BlockSpec((cols, width), lambda s, r: (dest(s, r), 0))],
        pl.BlockSpec((1, width, 4 * cols), lambda s, r: (s, 0, 0)),
        jax.ShapeDtypeStruct((4, width, 4 * cols), BF),
        cost=(0, 4 * width * cols * 24),
    )(ids, mixer_in, mixer_in, mixer_in, mixer_out)


class Feed:
    def __init__(self, hidden_all):
        tiles = hidden_all // 128 // 8
        self.half_at = 8 * tiles
        assert hidden_all == (8 * tiles + 4) * 128
        self.near = tiles * 128
        self.near_up = 2 * self.near + 128
        self.units = self.near + 128


def pack_feed(ids, gate_up, down, feed):
    width = gate_up.shape[1]
    near, up = feed.near, feed.near_up
    shapes = [(width, up), (near + 64, width)]

    def body(ids_ref, *refs):
        g_ref, u_ref, gh_ref, uh_ref, d_ref, dh_ref, out_ref, down_ref = refs
        odd = (ids_ref[0] ^ pl.program_id(0)) % 2
        out_ref[0, :, 0:near] = g_ref[0].astype(BF)
        lane = lax.broadcasted_iota(jnp.int32, (width, 128), 1)
        gh, uh = gh_ref[0], uh_ref[0]
        even_mix = jnp.where(lane < 64, gh, pltpu.roll(uh, 64, 1))
        odd_mix = jnp.where(lane < 64, pltpu.roll(gh, 64, 1), uh)
        out_ref[0, :, near : near + 128] = jnp.where(odd == 1, odd_mix, even_mix).astype(BF)
        out_ref[0, :, near + 128 : up] = u_ref[0].astype(BF)
        down_ref[0, 0:near] = d_ref[...].astype(BF)
        down_ref[0, near : near + 64] = dh_ref[...].astype(BF)

    def dest(s, r):
        return 4 * r[1] + (r[0] ^ s)

    def tile(s, r):
        return feed.half_at + 2 * r[1] + (r[0] ^ s) // 2

    def cols(i):
        return pl.BlockSpec((1, width, near), lambda s, r: (i, 0, dest(s, r)))

    def mix(i):
        return pl.BlockSpec((1, width, 128), lambda s, r: (i, 0, tile(s, r)))

    in_specs = [
        cols(0),
        cols(1),
        mix(0),
        mix(1),
        pl.BlockSpec((near, width), lambda s, r: (dest(s, r), 0)),
        pl.BlockSpec((64, width), lambda s, r: (2 * feed.half_at + dest(s, r), 0)),
    ]
    args = [gate_up, gate_up, gate_up, gate_up, down, down]
    return call(
        body,
        (4,),
        in_specs,
        [pl.BlockSpec((1, *shape), lambda s, r: (s, 0, 0)) for shape in shapes],
        [jax.ShapeDtypeStruct((4, *shape), BF) for shape in shapes],
        cost=(0, 4 * width * (up + near + 64) * 6),
    )(ids, *args)


def mp_perm(value, s):
    return lax.ppermute(value, "mp", [(i, i ^ s) for i in range(4)])


def rep_perm(value):
    return lax.ppermute(value, "rep", [(0, 1), (1, 0)])


def across_plane(packed):
    moved = [mp_perm(packed[s], s) for s in (1, 2, 3)]
    return jnp.concatenate([packed[0], *moved], axis=0), moved


def after(value, *others):
    return lax.optimization_barrier((value, *others))[0]


def from_earlier(value, count):
    return [
        lax.ppermute(value, "ctx", [(i, i + d) for i in range(count - d)]) for d in range(1, count)
    ]


def total_before(value, count):
    shift = 1
    total = lax.ppermute(value, "ctx", [(i, i + 1) for i in range(count - 1)])
    so_far = total + value
    while 2 * shift < count:
        came = lax.ppermute(so_far, "ctx", [(i, i + 2 * shift) for i in range(count - 2 * shift)])
        total, so_far, shift = total + came, so_far + came, 2 * shift
    return total


def normalise(table, token_pages, gain):
    _, page, width = token_pages.shape
    pages = table.shape[0]

    def body(table_ref, x_ref, g_ref, out_ref):
        x = x_ref[0].astype(F32)
        scale = lax.rsqrt(jnp.mean(x * x, axis=-1, keepdims=True) + EPS)
        out_ref[...] = (x * scale * g_ref[...]).astype(BF)

    return call(
        body,
        (pages,),
        [pl.BlockSpec((1, page, width), lambda i, t: (t[i], 0, 0)), whole((1, width))],
        pl.BlockSpec((page, width), lambda i, t: (i, 0)),
        jax.ShapeDtypeStruct((pages * page, width), BF),
        cost=(pages * page * width * 4, pages * page * width * 4),
    )(table, token_pages, gain.reshape(1, width))


def reset_counts(live_here, page_start, lengths, page):
    rows = live_here.shape[0] * page
    positions = (page_start[:, None] + jnp.arange(page, dtype=jnp.int32)[None, :]).reshape(rows)
    starts = jnp.cumsum(lengths) - lengths
    resets = (jnp.repeat(live_here, page) == 1) & jnp.any(positions[:, None] == starts[None, :], axis=1)
    count = jnp.cumsum(resets.astype(jnp.int32))
    cnt_col = count.reshape(rows, 1)
    cnt_row = count.reshape(-1, 1, page)
    last = count.reshape(-1, page)[:, -1]
    return cnt_col, cnt_row, last


def step_state(state, ks, v, same_last, keep, final):
    update = tn(v, jnp.where(same_last, ks, jnp.zeros_like(ks)))
    return (jnp.where(keep, state, 0.0) + update) * final


def project(ids, live, last, normed, foreign, weights, floor, cnt_col):
    width = normed.shape[1]
    cols = floor.shape[1]
    heads = cols // HEAD
    pages = live.shape[0]
    rows = cnt_col.shape[0]
    page = rows // pages
    group = 4
    steps = pages // group

    n = len(weights.arrays)

    def body(ids_ref, *refs):
        pl.when(ids_ref[2] == 1)(lambda: work(ids_ref, *refs))

    def work(ids_ref, live_ref, last_ref, x_ref, *refs):
        f_refs, refs = refs[: len(foreign)], refs[len(foreign) :]
        w_refs = refs[:n]
        fl_ref, cnt_ref, qs_ref, ks_ref, v_ref, fin_ref, st_ref, state, total, held, sems = refs[n:]
        step = pl.program_id(0)

        @pl.when(step == 0)
        def _():
            weights.start(ids_ref, w_refs, held, sems)
            state[...] = jnp.zeros_like(state)
            total[...] = jnp.zeros_like(total)
            weights.wait(ids_ref, w_refs, held, sems)

        x = x_ref[...]
        if foreign:
            core, y = ids_ref[0] & 1, ids_ref[0] >> 1
            tiles = []
            for q in range(group):
                near, far = ([f[:, 0, dy].reshape(page, width) for dy in range(2)] for f in f_refs)
                row = [jnp.where(core == q % 2, a, b) for a, b in zip(near, far)]
                tiles.append(jnp.where(y == q // 2, row[0], row[1]))
            x = jnp.where((step >> 1) == ids_ref[8], x, jnp.concatenate(tiles, axis=0))
        proj = nn(x, held[...])
        row = lax.broadcasted_iota(jnp.int32, (page, page), 0)
        col = lax.broadcasted_iota(jnp.int32, (page, page), 1)
        lower = (row >= col).astype(F32)
        floor_row = fl_ref[...]
        for j in range(group):
            p = step * group + j
            here = slice(j * page, (j + 1) * page)
            alive = live_ref[p].astype(F32)
            now = last_ref[p]
            before = jnp.where(p == 0, 0, last_ref[jnp.maximum(p - 1, 0)])
            q = proj[here, 0:cols]
            q = q * sigmoid(q)
            f = proj[here, cols : 2 * cols]
            gate = sigmoid(f)
            forget = floor_row + (1.0 - floor_row) * gate
            key = (1.0 - forget) * alive
            log_decay = jnp.log(forget) * alive
            cum = jnp.dot(lower, log_decay, precision=lax.Precision.HIGHEST, preferred_element_type=F32)
            final_log = cum[page - 1 : page, :]
            final = jnp.exp(final_log)
            ks = (key * jnp.exp(-cum)).astype(BF)
            v = proj[here, 2 * cols : 3 * cols].astype(BF)
            qs_ref[here, :] = (q * jnp.exp(cum)).astype(BF)
            ks_ref[here, :] = ks
            v_ref[here, :] = v
            fin_ref[j] = final
            total[...] += final_log
            same_last = cnt_ref[here, :] == now
            for h in range(heads):
                hc = slice(h * HEAD, (h + 1) * HEAD)
                state[h] = step_state(state[h], ks[:, hc], v[:, hc], same_last, now == before, final[:, hc])

        @pl.when(step == steps - 1)
        def _():
            none = last_ref[pages - 1] == 0
            decay = jnp.where(none, jnp.exp(total[...]), 0.0)
            for h in range(heads):
                st_ref[h, 0:HEAD, :] = state[h].astype(BF)
                st_ref[h, HEAD : HEAD + 16, :] = jnp.broadcast_to(
                    decay[:, h * HEAD : (h + 1) * HEAD], (16, HEAD)
                ).astype(BF)

    block = group * page
    return call(
        body,
        (steps,),
        [
            pl.BlockSpec((block, width), lambda i, *_: (i & 1, 0)),
        ]
        + [
            pl.BlockSpec(
                (2, 1, 2, page // 2, width), lambda i, r, *_: (0, (i & 1) ^ r[1], 0, 0, 0)
            )
        ]
        * len(foreign)
        + [ANY] * n
        + [
            whole((1, cols)),
            pl.BlockSpec((block, 1), lambda i, *_: (i, 0)),
        ],
        [
            pl.BlockSpec((block, cols), lambda i, *_: (i, 0)),
            pl.BlockSpec((block, cols), lambda i, *_: (i, 0)),
            pl.BlockSpec((block, cols), lambda i, *_: (i, 0)),
            pl.BlockSpec((group, 1, cols), lambda i, *_: (i, 0, 0)),
            whole((heads, HEAD + 16, HEAD)),
        ],
        [
            jax.ShapeDtypeStruct((rows, cols), BF),
            jax.ShapeDtypeStruct((rows, cols), BF),
            jax.ShapeDtypeStruct((rows, cols), BF),
            jax.ShapeDtypeStruct((pages, 1, cols), F32),
            jax.ShapeDtypeStruct((heads, HEAD + 16, HEAD), BF),
        ],
        scratch=[pltpu.VMEM((heads, HEAD, HEAD), F32), pltpu.VMEM((1, cols), F32), *weights.scratch],
        prefetch=3,
        cost=(2 * rows * width * 3 * cols, rows * width * 2 + width * cols * 8),
    )(ids, live, last, normed, *foreign, *weights.arrays, floor, cnt_col)


def mix(ids, last, earlier, qs, ks, v, fin, weights, cnt_col, cnt_row):
    rows, cols = qs.shape
    heads = cols // HEAD
    pages = fin.shape[0]
    page = rows // pages
    group = 4
    steps = pages // group
    width = weights.planes * weights.rows
    n = len(earlier)
    spans = steps // 2
    m = n + 4 + len(weights.arrays)

    def body(ids_ref, *refs):
        pl.when(ids_ref[2] == 1)(lambda: work(ids_ref, *refs))

    def work(ids_ref, last_ref, *refs):
        packs = refs[:n]
        qs_ref, ks_ref, v_ref, fin_ref = refs[n : n + 4]
        w_refs = refs[n + 4 : m]
        cc_ref, cr_ref = refs[m : m + 2]
        outs = refs[m + 2 : m + 2 + 2 * spans]
        state, held, sems = refs[m + 2 + 2 * spans :]
        step = pl.program_id(0)

        @pl.when(step == 0)
        def _():
            weights.start(ids_ref, w_refs, held, sems)
            for h in range(heads):
                total = jnp.zeros((HEAD, HEAD), F32)
                for pack in reversed(packs):
                    total = total * pack[h, HEAD : HEAD + 1, :].astype(F32) + pack[h, 0:HEAD, :].astype(F32)
                state[h] = total

        row = lax.broadcasted_iota(jnp.int32, (page, page), 0)
        col = lax.broadcasted_iota(jnp.int32, (page, page), 1)
        lower = row >= col
        normed = []
        for j in range(group):
            p = step * group + j
            here = slice(j * page, (j + 1) * page)
            now = last_ref[p]
            before = jnp.where(p == 0, 0, last_ref[jnp.maximum(p - 1, 0)])
            cc, cr = cc_ref[here, :], cr_ref[j]
            allowed = lower & (cc == cr)
            reached = cc == before
            same_last = cc == now
            for h in range(heads):
                hc = slice(h * HEAD, (h + 1) * HEAD)
                q_h, k_h, v_h = qs_ref[here, hc], ks_ref[here, hc], v_ref[here, hc]
                scores = jnp.where(allowed, nt(q_h, k_h), 0.0).astype(BF)
                out = nn(scores, v_h)
                out = out + jnp.where(reached, nt(q_h, state[h].astype(BF)), 0.0)
                state[h] = step_state(state[h], k_h, v_h, same_last, now == before, fin_ref[j, :, hc])
                scale = lax.rsqrt(jnp.mean(out * out, axis=-1, keepdims=True) + EPS)
                normed.append((out * scale).astype(BF))
        hn = jnp.concatenate(
            [jnp.concatenate(normed[j * heads : (j + 1) * heads], axis=1) for j in range(group)], axis=0
        )

        @pl.when(step == 0)
        def _():
            weights.wait(ids_ref, w_refs, held, sems)

        for dc in range(2):
            for dy in range(2):
                term = nt(hn, held[block_of(ids_ref[0] ^ (2 * dy + dc), width // 4), :]).astype(BF)
                for span in range(spans):

                    @pl.when((step // 2) ^ ids_ref[8] == span)
                    def _(span=span, dc=dc, dy=dy, term=term):
                        outs[2 * span + dc][:, 0, dy] = term.reshape(2, block // 2, width // 4)

    block = group * page
    rowspec = pl.BlockSpec((block, cols), lambda i, *_: (i, 0))

    def terms(span):
        def index(i, r, l):
            low = 2 * (span ^ r[8])
            i = jnp.minimum(jnp.maximum(i, low), low + 1) & 1
            return (0, i ^ r[1], 0, 0, 0)

        return pl.BlockSpec((2, 1, 2, block // 2, width // 4), index)

    return call(
        body,
        (steps,),
        [whole(e.shape) for e in earlier]
        + [
            rowspec,
            rowspec,
            rowspec,
            pl.BlockSpec((group, 1, cols), lambda i, *_: (i, 0, 0)),
        ]
        + [ANY] * len(weights.arrays)
        + [
            pl.BlockSpec((block, 1), lambda i, *_: (i, 0)),
            pl.BlockSpec((group, 1, page), lambda i, *_: (i, 0, 0)),
        ],
        [terms(span) for span in range(spans) for _ in range(2)],
        [jax.ShapeDtypeStruct((2, 2, 2, block // 2, width // 4), BF)] * (2 * spans),
        scratch=[pltpu.VMEM((heads, HEAD, HEAD), F32), *weights.scratch],
        prefetch=2,
        cost=(2 * rows * cols * width, rows * width * 2),
    )(ids, last, *earlier, qs, ks, v, fin, *weights.arrays, cnt_col, cnt_row)


def add(a, b):
    return (a.astype(F32) + b.astype(F32)).astype(BF)


def sum_scatter(terms, *others):
    mine, other = terms[0], mp_perm(terms[1], 1)
    a_keep, a_send = add(mine[0, 0], other[0, 0]), add(mine[0, 1], other[0, 1])
    b_keep, b_send = add(mine[1, :, 0], other[1, :, 0]), add(mine[1, :, 1], other[1, :, 1])
    a_came, b_came = rep_perm(a_send), mp_perm(b_send, 2)
    a_came = after(a_came, *others)
    a_send, b_send = add(a_keep[1], a_came[1]), add(b_keep[1], b_came[1])
    a_last, b_last = mp_perm(a_send, 2), rep_perm(b_send)
    a = a_keep[0].astype(F32) + a_came[0].astype(F32) + a_last.astype(F32)
    b = b_keep[0].astype(F32) + b_came[0].astype(F32) + b_last.astype(F32)
    return jnp.concatenate([a, b], axis=0), (a_came, b_came)


def gather_core(value):
    half = value.shape[0] // 2
    a, b = value[:half], value[half:]
    a_y, b_x = mp_perm(a, 2), rep_perm(b)
    a_pair, b_pair = jnp.stack([a, a_y]), jnp.stack([b, b_x])
    a_x, b_y = rep_perm(a_pair), mp_perm(b_pair, 2)
    return jnp.stack([jnp.stack([a_pair, a_x]), jnp.stack([b_pair, b_y], axis=1)])


def gather_pieces(value):
    half = value.shape[0] // 2
    a, b = value[:half], value[half:]
    a_y, b_x = mp_perm(a, 2), rep_perm(b)
    a_pair, b_pair = jnp.stack([a, a_y]), jnp.stack([b, b_x])
    a_x, b_y = rep_perm(a_pair), mp_perm(b_pair, 2)
    mine = [a_pair, a_x, b_pair, b_y]
    return [*mine, *(mp_perm(piece, 1) for piece in mine)]


def block_of(k, rows):
    return pl.ds(pl.multiple_of(k * rows, rows), rows)


def feed_up(ids, pieces, gain, weights, feed):
    near, up, units = feed.near, feed.near_up, feed.units
    rows, kwide = pieces[0].shape[-2:]
    width = 4 * kwide
    n = len(weights.arrays)
    places = [(dy, dc) for dy in range(2) for dc in range(2)]

    def body(ids_ref, *rest):
        p_refs, g_ref, w_refs = rest[:8], rest[8], rest[9 : 9 + n]
        out_ref, x_ref, held, sems = rest[9 + n :]
        dx = pl.program_id(0)
        pl.when(dx == 0)(lambda: weights.start(ids_ref, w_refs, held, sems))
        for ab in range(2):
            blocks = []
            for dy, dc in places:
                first, second, third, fourth = p_refs[4 * dc : 4 * dc + 4]
                if ab == 0:
                    blocks.append(jnp.where(dx == 0, first[dy], second[dy]).astype(F32))
                else:
                    blocks.append((third, fourth)[dy][0].astype(F32))
            square = sum(jnp.sum(b * b, axis=-1, keepdims=True) for b in blocks)
            scale = lax.rsqrt(square / width + EPS)
            for (dy, dc), b in zip(places, blocks):
                k = ids_ref[0] ^ (2 * dy + dc)
                x_ref[ab, :, block_of(k, kwide)] = (b * scale * g_ref[k]).astype(BF)
        pl.when(dx == 0)(lambda: weights.wait(ids_ref, w_refs, held, sems))

        for ab in range(2):
            h = nn(x_ref[ab], held[...])
            gate, edge, upward = h[:, 0:near], h[:, near : near + 128], h[:, near + 128 : up]
            out_ref[ab, 0, :, 0:near] = (gate * sigmoid(gate) * upward).astype(BF)
            mixed = edge * sigmoid(edge) * pltpu.roll(edge, 64, 1)
            lane = lax.broadcasted_iota(jnp.int32, mixed.shape, 1)
            out_ref[ab, 0, :, near:units] = jnp.where(lane < 64, mixed, 0.0).astype(BF)

    pair = whole((2, rows, kwide))
    one = pl.BlockSpec((1, rows, kwide), lambda i, r: (i, 0, 0))
    return call(
        body,
        (2,),
        [pair, pair, one, one] * 2 + [whole(gain.shape)] + [ANY] * n,
        pl.BlockSpec((2, 1, rows, units), lambda i, r: (0, i, 0, 0)),
        jax.ShapeDtypeStruct((2, 2, rows, units), BF),
        scratch=[pltpu.VMEM((2, rows, width), BF), *weights.scratch],
        cost=(8 * rows * width * up, width * up * 2 + 16 * rows * width),
        limit=FEED_LIMIT,
    )(ids, *pieces, gain, *weights.arrays)


def feed_down(ids, hidden, weights, kwide, dc):
    rows, units = hidden.shape[-2:]
    used = units - 64
    parts = 4 if weights.ndim == 3 else 1

    def body(ids_ref, h_ref, w_ref, out_ref, held, sems):
        def copies():
            for dy in range(2):
                k = ids_ref[0] ^ (2 * dy + dc)
                for s in range(parts):
                    if parts == 1:
                        ref, to = w_ref.at[:, block_of(k, kwide)], dy * kwide
                    else:
                        ref = w_ref.at[k, pl.ds(s * used, used)]
                        to = pl.multiple_of(dy * kwide + (ids_ref[0] ^ s) * (kwide // 4), 128)
                    to = held.at[pl.ds(0, used), pl.ds(to, kwide // parts)]
                    yield pltpu.make_async_copy(ref, to, sems.at[parts * dy + s])

        @pl.when(pl.program_id(0) == 0)
        def _():
            for copy in copies():
                copy.start()
            held[used:units, :] = jnp.zeros((units - used, 2 * kwide), BF)
            for copy in copies():
                copy.wait()

        term = nn(h_ref[0, 0], held[...]).astype(BF)
        for dy in range(2):
            out_ref[0, 0, dy] = term[:, dy * kwide : (dy + 1) * kwide]

    return call(
        body,
        (4,),
        [pl.BlockSpec((1, 1, rows, units), lambda i, r: (i % 2, i // 2, 0, 0)), ANY],
        pl.BlockSpec((1, 1, 2, rows, kwide), lambda i, r: (i % 2, i // 2, 0, 0, 0)),
        jax.ShapeDtypeStruct((2, 2, 2, rows, kwide), BF),
        scratch=[pltpu.VMEM((units, 2 * kwide), BF), pltpu.SemaphoreType.DMA((2 * parts,))],
        cost=(16 * rows * kwide * units, 4 * kwide * units + 16 * rows * kwide),
    )(ids, hidden, weights)


def shards(
    token_pages,
    page_table,
    live_flags,
    lengths,
    decay_floor,
    mixer_gain,
    feed_gain,
    trainer_mixer_in,
    trainer_mixer_out,
    trainer_gate_up,
    trainer_down,
):
    ctx_count = lax.axis_size("ctx")
    ctx_index = lax.axis_index("ctx")
    mp_index = lax.axis_index("mp")
    rep_index = lax.axis_index("rep")
    pages, page, width = token_pages.shape
    cols = decay_floor.shape[0]
    kwide = width // 4
    feed = Feed(trainer_gate_up.shape[2])
    line = ctx_count == 4 and pages == 8
    middle = (ctx_index == 1) | (ctx_index == 2)
    beyond = jnp.where(ctx_index == 1, 0, 3)
    order = [ctx_index, 3 - ctx_index, beyond, 3 - beyond]
    own_span = (ctx_index == 1).astype(jnp.int32) if line else 0
    active = middle.astype(jnp.int32) if line else 1
    sources = [ctx_index, ctx_index ^ 1, ctx_index ^ jnp.where(middle, 3, 2), ctx_index ^ jnp.where(middle, 2, 3)]
    ids = jnp.stack([mp_index, rep_index, active, *order, ctx_index, own_span, *sources]).astype(jnp.int32)

    def gather(value):
        return Rows([lax.all_gather(value, "ctx", axis=0)])

    packed_mixer = pack_mixer(ids, trainer_mixer_in, trainer_mixer_out)
    plane_mixer, moved = across_plane(packed_mixer)
    flags = after(live_flags, packed_mixer)
    if line:
        sent = lax.dynamic_slice_in_dim(page_table, rep_index * 4 + mp_index, 1, 0)
        chunk = normalise(after(sent, packed_mixer), token_pages, mixer_gain)
        spread = jnp.broadcast_to(flags[:, None], (pages, 128)).astype(jnp.int32)
        came = lax.ppermute(spread, "ctx", [(0, 1), (3, 2)])
        chunk = after(chunk, came)
        ids_feed = after(ids, chunk)
        chunk = lax.ppermute(chunk, "ctx", [(0, 1), (3, 2)])
        packed_up, packed_down = pack_feed(ids_feed, trainer_gate_up, trainer_down, feed)
        plane_up, moved_up = across_plane(after(packed_up, *moved))
        plane_down, _ = across_plane(after(packed_down, *moved_up))
        totals = jnp.broadcast_to(jnp.sum(spread + came, axis=0, keepdims=True), (8, 128))
        totals = lax.ppermute(totals, "ctx", [(1, 2)])
        base = after(totals, plane_mixer)[0, 0]
        theirs = came[:, 0]
        live_here = jnp.concatenate(
            [jnp.where(ctx_index == 1, theirs, flags), jnp.where(ctx_index == 1, flags, theirs)]
        )
        page_start = (base + jnp.cumsum(live_here) - live_here) * page

        plane_mixer = after(plane_mixer, came, totals, packed_up, packed_down, chunk)
        across = lax.ppermute(plane_mixer, "ctx", [(1, 2), (2, 1)])
        inward = lax.ppermute(plane_mixer, "ctx", [(0, 1), (3, 2)])
        normed = normalise(after(page_table, plane_mixer), token_pages, mixer_gain)
        counts = reset_counts(live_here, page_start, after(lengths, plane_mixer), page)
        mine = gather_core(chunk)
        across, inward, normed, counts, mine = lax.optimization_barrier(
            (across, inward, normed, counts, mine)
        )
        onward = lax.ppermute(inward, "ctx", [(1, 2), (2, 1)])
        mixer_rows = [plane_mixer, across, inward, onward]
        plane_up = after(plane_up, onward)
        foreign = (mine, mp_perm(mine, 1))
    else:
        packed_up, packed_down = pack_feed(ids, trainer_gate_up, trainer_down, feed)
        plane_up, moved_up = across_plane(after(packed_up, *moved))
        plane_down, _ = across_plane(after(packed_down, *moved_up))
        normed = normalise(page_table, token_pages, mixer_gain)
        foreign = ()
        live_here = flags
        live_total = jnp.broadcast_to(jnp.sum(flags) * page, (8, 128)).astype(jnp.int32)
        page_start = total_before(live_total, ctx_count)[0, 0] + (jnp.cumsum(flags) - flags) * page
        counts = reset_counts(live_here, page_start, lengths, page)
        mixer_rows = gather(plane_mixer).arrays
    cnt_col, cnt_row, last = counts
    w_up = gather(plane_up)
    w_down = lax.all_gather(plane_down, "ctx", axis=0)
    if kwide // 4 % 128 or ctx_count != 4:
        parts = w_down.reshape(ctx_count, 4, -1, w_down.shape[-1])
        parts = jnp.take(parts, mp_index ^ jnp.arange(4), axis=1)
        w_down = jnp.transpose(parts, (2, 0, 1, 3)).reshape(-1, width)

    w_in, w_out = Rows(mixer_rows, 0, 3 * cols), Rows(mixer_rows, 3 * cols)

    half_rows = pages * page // 2
    table_half = lax.dynamic_slice_in_dim(page_table, rep_index * (pages // 2), pages // 2, 0)
    token_cols = lax.dynamic_slice_in_dim(token_pages, mp_index * kwide, kwide, 2)
    ordered = jnp.take(token_cols, table_half, axis=0).reshape(half_rows, kwide)

    qs, ks, v, fin, pack = project(
        ids, live_here, last, normed, foreign, w_in, decay_floor.reshape(1, cols), cnt_col
    )
    if line:
        earlier = [lax.ppermute(pack, "ctx", [(1, 2)])]
    else:
        earlier = from_earlier(pack, ctx_count)
    terms = mix(ids, last, earlier, qs, ks, v, fin, w_out, cnt_col, cnt_row)
    if line:
        theirs, stage = sum_scatter(terms[2:])
        back = lax.ppermute(theirs.astype(BF), "ctx", [(1, 0), (2, 3)])
        keep, send, *_ = lax.optimization_barrier((terms[0], terms[1], *stage))
        mixed = jnp.where(middle, sum_scatter((keep, send))[0], back.astype(F32))
    else:
        mixed = sum_scatter(terms)[0]
    residual = ordered.astype(F32) + mixed
    pieces = gather_pieces(residual.astype(BF))
    hidden = feed_up(ids, pieces, feed_gain.reshape(4, 1, kwide), w_up, feed)
    send = feed_down(ids, hidden, w_down, kwide, 1)
    summed = residual + sum_scatter((feed_down(ids, hidden, w_down, kwide, 0), send))[0]
    live_half = jnp.repeat(
        lax.dynamic_slice_in_dim(live_flags, rep_index * (pages // 2), pages // 2, 0), page
    )
    return jnp.where(live_half[:, None] == 1, summed, 0.0).astype(BF)


def solution(mesh):
    in_specs = (
        P("ctx", None, None),
        P("ctx"),
        P("ctx"),
        P(),
        P(("mp", "rep")),
        P(),
        P(),
        P(None, ("ctx", "mp"), None),
        P(None, ("ctx", "mp")),
        P(None, ("ctx", "mp"), None),
        P(None, ("ctx", "mp")),
    )
    out_specs = P(("ctx", "rep"), "mp")
    return jax.shard_map(shards, mesh=mesh, in_specs=in_specs, out_specs=out_specs, check_vma=False)
```
